128 devices in a mesh: expert: 32 (over x, z, y_lo), zero: 4 (over y_hi, core).
Axes of the slice: x: 4, y: 4 (y_hi: 2, y_lo: 2; y = y_hi * 2 + y_lo), z: 4, core: 2. Of those that a mesh axis runs over, the one named last changes fastest.
Arguments:
- tokens: bfloat16 [24576, 4096], P(('expert', 'zero')), may hold values from -6 to 6
- expert_ids: int32 [24576, 8], P(('expert', 'zero')), may hold values from 0 to 127, all different within a row; in each aligned block of 192 rows (0 to 191, 192 to 383, ...) at most 24 rows name the same one
- route_weights: bfloat16 [24576, 8], P(('expert', 'zero')), may hold values from 0.049804688 to 0.5
- master_gu: float32 [32, 4096, 1536], P('expert', 'zero'), may hold values from -0.09375 to 0.09375
- grad_gu: bfloat16 [32, 4096, 1536], P('expert', 'zero'), may hold values from -0.015625 to 0.015625
- first_gu: bfloat16 [32, 4096, 1536], P('expert', 'zero'), may hold values from -0.015625 to 0.015625
- second_gu: bfloat16 [32, 4096, 1536], P('expert', 'zero'), may hold values from 9.9651515e-08 to 9.953976e-06
- master_down: float32 [32, 4096, 768], P('expert', 'zero'), may hold values from -0.21875 to 0.21875
- grad_down: bfloat16 [32, 4096, 768], P('expert', 'zero'), may hold values from -0.015625 to 0.015625
- first_down: bfloat16 [32, 4096, 768], P('expert', 'zero'), may hold values from -0.015625 to 0.015625
- second_down: bfloat16 [32, 4096, 768], P('expert', 'zero'), may hold values from 9.9651515e-08 to 9.953976e-06
Outputs:
- mixed: bfloat16 [24576, 4096], P(('expert', 'zero'))
The draws below stay inside these ranges and needn't reach their ends.
Inputs may be any that keep to these rules, and one draw needn't show every extreme that they name: `expert_ids`: each row names 8 different experts; within the 192 rows of one device no expert is named more than 24 times, a bound that some block reaches.
All inputs are finite; a program needn't handle non-finite values.
Results may differ from the reference program's by a relative error of at most 0.003.
The reference program's roundings to bfloat16 on the way count: a program that leaves them out, or rounds other values in their place, can miss the bound.
Values may be sent and summed in bfloat16 or wider, within the bound.
A program may use at most 256 MiB of HBM per device.

```python
import math
import jax
import jax.numpy as jnp
import numpy as np
from jax import lax

D = 4096
EXPERTS = 128
TOP = 8
HW = 768
TOK_DEV = 192
CAP = 24
FLIGHT = 32
TOKENS = 24576
N_EXPERT = 32
N_ZERO = 4


def levels(stream_key, dims, shards, least, high):
    loudness = 1.0
    for dim, blocks in shards:
        steps = jax.random.uniform(jax.random.fold_in(jax.random.fold_in(stream_key, 6), dim), (blocks,), jnp.float32, least / len(shards), high / len(shards))
        loudness = loudness * jnp.repeat(jnp.exp(steps), dims[dim] // blocks).reshape((-1,) + (1,) * (len(dims) - 1 - dim))
    return loudness


def shared_out(own_key, own, number, rows, number_of, top, bound, skew):
    ranking = jax.random.permutation(own_key, number_of)
    heavy_load, ordinary = shares(number_of, rows * top, bound, skew, True), shares(number_of, rows * top, bound, skew, False)
    places = jnp.arange(number_of)

    def named(sizes, offset_by):
        used = int((sizes > 0).sum())
        fixed = max(1, used // 4)
        passed = fixed + (places - fixed + offset_by * (used - fixed)) % max(1, number_of - fixed)
        return jnp.zeros((number_of,), jnp.int32).at[ranking[jnp.where(places < fixed, places, passed)]].set(jnp.asarray(sizes, jnp.int32))

    sizes = jnp.where(number % 4 == 0, named(heavy_load, number // 4), named(ordinary, number - number // 4 - 1))
    mixed = jax.random.permutation(jax.random.fold_in(own, 3), number_of)
    giver, receiver = mixed[0:number_of // 2 * 2:2], mixed[1:number_of // 2 * 2:2]
    slack = jnp.minimum(sizes[giver] - 1, bound - sizes[receiver]) // 2
    slack = jnp.where((giver == ranking[0]) | (receiver == ranking[0]) | (sizes[receiver] == 0), 0, jnp.maximum(slack, 0))
    passed = jax.random.randint(jax.random.fold_in(own, 4), (number_of // 2,), 0, 1 << 20) % (slack + 1)
    sizes = sizes.at[giver].add(-passed).at[receiver].add(passed)
    members = jnp.searchsorted(jnp.cumsum(sizes), jnp.arange(rows * top), side="right").astype(jnp.int32)
    table = members.reshape(top, rows).T
    table = table[jax.random.permutation(jax.random.fold_in(own, 1), rows)]
    offset_by = jax.random.randint(jax.random.fold_in(own, 2), (rows, 1), 0, top)
    return jnp.take_along_axis(table, (jnp.arange(top)[None, :] + offset_by) % top, axis=1)


def shares(amount, total, reach, slope, full):
    weights = [(1 << 20) // math.isqrt(standing ** slope) + 1 for standing in range(1, amount + 1)]
    largest = reach if full else min(reach, max(-(-total // amount), total * weights[0] // sum(weights)))
    least = 1 if total - largest >= amount - 1 else 0
    counts, surplus = [largest] + [least] * (amount - 1), total - largest - least * (amount - 1)
    while surplus > 0:
        movable = [i for i in range(1, amount) if counts[i] < largest] or [i for i in range(1, amount) if counts[i] < reach]
        whole, remaining = sum([weights[i] for i in movable]), surplus
        for i in movable:
            more = min(reach - counts[i], max(1, remaining * weights[i] // whole), surplus)
            counts[i] = counts[i] + more
            surplus = surplus - more
    return np.array(counts)


def noise(rng, shape, scale, limit, cuts=(), held_as=jnp.bfloat16):
    gain = levels(rng, shape, cuts, -0.22, 0.18) if cuts else 1.0
    entries = jax.random.normal(rng, shape, jnp.float32) * scale * gain
    return jnp.minimum(jnp.maximum(entries, -limit), limit).astype(held_as)


def setup_inputs(seed: int = 0) -> dict:
    keys = jax.random.split(jax.random.key(seed), 12)
    tokens = noise(keys[0], (TOKENS, D), 1.0, 6.0, ((0, 128),))
    expert_ids_keys = jax.random.split(jax.random.fold_in(keys[1], 1), TOKENS // TOK_DEV)
    expert_ids_turns = jax.random.permutation(jax.random.fold_in(keys[1], 3), TOKENS // TOK_DEV)
    expert_ids = jax.vmap(lambda own, number: shared_out(jax.random.fold_in(keys[1], 2), own, number, TOK_DEV, EXPERTS, TOP, CAP, 2))(expert_ids_keys, expert_ids_turns).reshape((TOKENS, TOP))
    route_weights = jnp.clip(jnp.exp(math.log(0.5) - 2.306499 * jax.random.uniform(keys[2], (TOKENS, TOP), jnp.float32) ** levels(keys[2], (TOKENS, TOP), ((0, 128),), -0.2, 0.2)), 0.049804688, 0.5).astype(jnp.bfloat16)
    master_gu = noise(keys[3], (FLIGHT, D, 2 * HW), D ** -0.5, 0.09375, ((0, 32), (1, 4)), jnp.float32)
    grad_gu = noise(keys[4], (FLIGHT, D, 2 * HW), 0.001, 0.015625, ((0, 32), (1, 4)))
    first_gu = noise(keys[5], (FLIGHT, D, 2 * HW), 0.001, 0.015625, ((0, 32), (1, 4)))
    second_gu = jnp.clip(jnp.exp(math.log(9.953975677490234e-06) - 4.6040481 * jax.random.uniform(keys[6], (FLIGHT, D, 2 * HW), jnp.float32) ** levels(keys[6], (FLIGHT, D, 2 * HW), ((0, 32), (1, 4)), -0.2, 0.2)), 9.96515154838562e-08, 9.953975677490234e-06).astype(jnp.bfloat16)
    master_down = noise(keys[7], (FLIGHT, D, HW), HW ** -0.5, 0.21875, ((0, 32), (1, 4)), jnp.float32)
    grad_down = noise(keys[8], (FLIGHT, D, HW), 0.001, 0.015625, ((0, 32), (1, 4)))
    first_down = noise(keys[9], (FLIGHT, D, HW), 0.001, 0.015625, ((0, 32), (1, 4)))
    second_down = jnp.clip(jnp.exp(math.log(9.953975677490234e-06) - 4.6040481 * jax.random.uniform(keys[10], (FLIGHT, D, HW), jnp.float32) ** levels(keys[10], (FLIGHT, D, HW), ((0, 32), (1, 4)), -0.2, 0.2)), 9.96515154838562e-08, 9.953975677490234e-06).astype(jnp.bfloat16)
    return {"tokens": tokens, "expert_ids": expert_ids, "route_weights": route_weights, "master_gu": master_gu, "grad_gu": grad_gu, "first_gu": first_gu, "second_gu": second_gu, "master_down": master_down, "grad_down": grad_down, "first_down": first_down, "second_down": second_down}


beta_one = 0.9
beta_two = 0.999
learn_rate = 0.002
adam_eps = 1e-08
corr_one = 1.0
corr_two = 0.63230457523

def adam_step(master, gradient, moment_one, moment_two):
    grads = gradient.astype(jnp.float32)
    first = beta_one * moment_one.astype(jnp.float32) + (1.0 - beta_one) * grads
    second = beta_two * moment_two.astype(jnp.float32) + (1.0 - beta_two) * grads * grads
    return master - learn_rate * (first / corr_one) / (jnp.sqrt(second / corr_two) + adam_eps)

def block_cast(weights):
    lead = weights.shape[:-2]
    height, breadth = weights.shape[-2:]
    blocks = weights.reshape(lead + (height // 128, 128, breadth // 128, 128))
    largest = lax.optimization_barrier(jnp.max(jnp.abs(blocks), axis=(-3, -1)))
    scales = ((largest + 1e-06) / 448.0).astype(jnp.bfloat16)
    quantized = (blocks / scales.astype(jnp.float32)[..., :, None, :, None]).astype(jnp.bfloat16)
    return (quantized.reshape(weights.shape), scales)

def promoted_in(inputs, quantized, scales):
    count = inputs.shape[0]
    depth, outward = quantized.shape
    groups = depth // 128
    pieces = jnp.einsum('nkc,kcm->knm', inputs.reshape(count, groups, 128).astype(jnp.float32), quantized.reshape(groups, 128, outward).astype(jnp.float32))
    factor = jnp.repeat(scales.astype(jnp.float32), 128, axis=1)
    return lax.optimization_barrier(jnp.sum(pieces * factor[:, None, :], axis=0))

def promoted_out(hidden, quantized, scales):
    count = hidden.shape[0]
    outward, depth = quantized.shape
    groups = depth // 128
    pieces = jnp.einsum('nkc,mkc->knm', hidden.reshape(count, groups, 128).astype(jnp.float32), quantized.reshape(outward, groups, 128).astype(jnp.float32))
    factor = jnp.repeat(scales.astype(jnp.float32).T, 128, axis=1)
    return lax.optimization_barrier(jnp.sum(pieces * factor[:, None, :], axis=0))

def reference(tokens, expert_ids, route_weights, master_gu, grad_gu, first_gu, second_gu, master_down, grad_down, first_down, second_down):
    devices = N_EXPERT * N_ZERO
    local = EXPERTS // N_EXPERT
    quant_gu, scale_gu = block_cast(adam_step(master_gu, grad_gu, first_gu, second_gu))
    quant_down, scale_down = block_cast(adam_step(master_down, grad_down, first_down, second_down))
    paired = expert_ids.reshape(devices, TOK_DEV * TOP)
    onehot = (paired[:, :, None] == jnp.arange(EXPERTS, dtype=jnp.int32)[None, None, :]).astype(jnp.int32)
    before = jnp.cumsum(onehot, axis=1) - onehot
    slots = lax.optimization_barrier(jnp.sum(before * onehot, axis=2)).astype(jnp.int32).reshape(TOKENS, TOP)
    device_of = (jnp.arange(TOKENS, dtype=jnp.int32) // TOK_DEV).astype(jnp.int32)
    capacity = devices * CAP

    def one_expert(total, packed):
        q_gate, s_gate, q_down, s_down, index = packed
        expert = index * local
        chosen = expert_ids == expert
        matched = jnp.any(chosen, axis=1)
        position = jnp.where(matched, device_of * CAP + lax.optimization_barrier(jnp.sum(jnp.where(chosen, slots, 0), axis=1)), capacity).astype(jnp.int32)
        buffer = jnp.zeros((capacity, D), jnp.bfloat16).at[position].set(tokens, mode='drop')
        gated = promoted_in(buffer, q_gate, s_gate)
        hidden = (jax.nn.silu(gated[:, :HW]) * gated[:, HW:]).astype(jnp.bfloat16)
        output = promoted_out(hidden, q_down, s_down).astype(jnp.bfloat16)
        picked = output[jnp.minimum(position, capacity - 1)].astype(jnp.float32)
        weight = lax.optimization_barrier(jnp.sum(jnp.where(chosen, route_weights.astype(jnp.float32), 0.0), axis=1))
        return (total + weight[:, None] * picked, None)
    start = jnp.zeros((TOKENS, D), jnp.float32)
    total, unused = lax.scan(one_expert, start, (quant_gu, scale_gu, quant_down, scale_down, jnp.arange(N_EXPERT, dtype=jnp.int32)))
    return total.astype(jnp.bfloat16)
```

```python
import jax
import jax.numpy as jnp
from jax import lax
from jax.experimental import pallas as pl
from jax.experimental.pallas import tpu as pltpu
from jax.sharding import PartitionSpec as P

MESH = pl.DeviceIdType.MESH
F32 = jnp.float32
BF16 = jnp.bfloat16

TOK = 192
D = 4096
CAP = 24
PAIR = 2 * CAP
PLANE = 16
ROWS = PLANE * PAIR
GU = 1536
HW = 768
SHARD = 1024
CHUNKS = 4
DC = D // CHUNKS
PARTS = 4
PART = SHARD // PARTS

beta_one = 0.9
beta_two = 0.999
learn_rate = 0.002
adam_eps = 1e-08
corr_two = 0.63230457523

OFFSETS = (
    (2, 2), (1, 2), (3, 2), (2, 1), (2, 3), (1, 1), (3, 3), (1, 3), (3, 1),
    (2, 0), (0, 2), (1, 0), (3, 0), (0, 1), (0, 3),
)
PEERS = len(OFFSETS)


def remote(src, dst, send_sem, recv_sem, device):
    return pltpu.make_async_remote_copy(
        src_ref=src,
        dst_ref=dst,
        send_sem=send_sem,
        recv_sem=recv_sem,
        device_id=device,
        device_id_type=MESH,
    )


def chunk_of(zero, k):
    sibling = zero + 1 - 2 * (zero % 2)
    base = sibling if k % 2 else zero
    return (base + 2) % 4 if k >= 2 else base


def adam(master, grad, first, second):
    grads = grad.astype(F32)
    m_one = beta_one * first.astype(F32) + (1.0 - beta_one) * grads
    m_two = beta_two * second.astype(F32) + (1.0 - beta_two) * grads * grads
    return master - learn_rate * m_one / (jnp.sqrt(m_two * (1.0 / corr_two)) + adam_eps)


def cast_block(block):
    largest = jnp.max(jnp.max(jnp.abs(block), axis=0, keepdims=True), axis=1, keepdims=True)
    scale = ((largest + 1e-06) / 448.0).astype(BF16).astype(F32)
    return (block * (1.0 / scale)).astype(BF16), scale


def kernel(
    tokens, ids, weights,
    mgu, ggu, fgu, vgu, mdn, gdn, fdn, vdn,
    out,
    tokv, pk, pks, sel, comb, og, xr, wgu, wdn, scg, scd, acc, hid, ret, ps, pr,
    am, ag, af, av, bm, bg, bf, bv,
    tok_l, tok_s, tok_r, pk_s, pk_r, dis_l, dis_s, dis_r, ret_l, ret_s, ret_r,
    wg_s, wg_r, wd_s, wd_r, sc_s, sc_r, par_s, par_r, a_sem, b_sem, out_sem,
):
    expert = lax.axis_index("expert")
    zero = lax.axis_index("zero")
    x, zz, yl = expert // 8, (expert // 2) % 4, expert % 2
    yh, core = zero // 2, zero % 2
    y = yh * 2 + yl
    pe = x * 4 + zz
    step = 1 - 2 * core

    def at(px, py, pz, pc):
        return (px * 8 + pz * 2 + py % 2, (py // 2) * 2 + pc)

    y_to, y_from = (y + step + 4) % 4, (y - step + 4) % 4
    to_dev = at(x, y_to, zz, core)
    from_dev = at(x, y_from, zz, core)
    sib_dev = at(x, y, zz, 1 - core)
    far_dev = at(x, (y + 2) % 4, zz, core)
    zero_to = (y_to // 2) * 2 + core

    peers = []
    sources = []
    for dx, dz in OFFSETS:
        px, pz = (x + dx) % 4, (zz + dz) % 4
        qx, qz = (x + 4 - dx) % 4, (zz + 4 - dz) % 4
        peers.append((at(px, y, pz, core), px * 4 + pz))
        sources.append(qx * 4 + qz)

    def slot_rows(p):
        return pl.ds(pl.multiple_of(p * PAIR, 16), PAIR)

    def columns(zero_index, k):
        return pl.ds(pl.multiple_of(chunk_of(zero_index, k) * DC, DC), DC)

    own_tok = []
    for k in range(CHUNKS):
        copy = pltpu.make_async_copy(
            tokens.at[:, columns(zero, k)], tokv.at[k, pl.ds(0, TOK)], tok_l.at[k]
        )
        copy.start()
        own_tok.append(copy)

    def gu_loads(chunk):
        slot = chunk % 2
        rows = pl.ds(pl.multiple_of(chunk * 128, 128), 128)
        return [
            pltpu.make_async_copy(src.at[0, rows], dst.at[slot], a_sem.at[slot, i])
            for i, (src, dst) in enumerate(((mgu, am), (ggu, ag), (fgu, af), (vgu, av)))
        ]

    def dn_loads(chunk):
        slot = chunk % 2
        rows = pl.ds(pl.multiple_of(chunk * 128, 128), 128)
        return [
            pltpu.make_async_copy(src.at[0, rows], dst.at[slot], b_sem.at[slot, i])
            for i, (src, dst) in enumerate(((mdn, bm), (gdn, bg), (fdn, bf), (vdn, bv)))
        ]

    for chunk in range(2):
        for copy in gu_loads(chunk):
            copy.start()
    for chunk in range(2):
        for copy in dn_loads(chunk):
            copy.start()

    lane = lax.broadcasted_iota(jnp.int32, (TOK, 128), 1)
    mine = jnp.zeros((TOK, 128), F32)
    theirs = jnp.zeros((TOK, 128), F32)
    for k in range(8):
        named = ids[:, k : k + 1]
        weight = weights[:, k : k + 1].astype(F32)
        for other in range(2):
            row = yl if other == 0 else 1 - yl
            value = jnp.where(
                named == lane * 8 + 4 * row,
                weight,
                jnp.where(named == (lane - 64) * 8 + 4 * row, 1.0, 0.0),
            )
            if other == 0:
                mine = mine + value
            else:
                theirs = theirs + value
    pk[0:TOK, :] = mine
    pks[...] = theirs

    barrier = pltpu.get_barrier_semaphore()
    greeted = [dev for dev, _ in peers] + [sib_dev, far_dev, to_dev, from_dev]
    for dev in greeted:
        pl.semaphore_signal(barrier, inc=1, device_id=dev, device_id_type=MESH)
    pl.semaphore_wait(barrier, len(greeted))

    sends = []

    def start(copy):
        copy.start()
        sends.append(copy)
        return copy

    pk_copy = start(remote(pks, pk.at[pl.ds(TOK, TOK)], pk_s, pk_r, to_dev))
    tok_copy = [
        start(
            remote(
                tokens.at[:, columns(zero_to, k)],
                tokv.at[k, pl.ds(TOK, TOK)],
                tok_s.at[k],
                tok_r.at[k],
                to_dev,
            )
        )
        for k in range(CHUNKS)
    ]

    eighth = lax.broadcasted_iota(jnp.int32, (8, 128), 0)
    scg[0] = jnp.zeros((8, GU), F32)
    scd[0] = jnp.zeros((8, SHARD), F32)

    def adam_gu(chunk, carry):
        slot = chunk % 2
        for copy in gu_loads(chunk):
            copy.wait()
        rows = pl.ds(pl.multiple_of(chunk * 128, 128), 128)

        def column_pair(n, inner):
            cols = pl.ds(pl.multiple_of(n * 256, 256), 256)
            fresh = adam(am[slot, :, cols], ag[slot, :, cols], af[slot, :, cols], av[slot, :, cols])
            for h in range(2):
                quant, scale = cast_block(fresh[:, h * 128 : h * 128 + 128])
                half = pl.ds(pl.multiple_of(n * 256 + h * 128, 128), 128)
                wgu[0, rows, half] = quant
                scg[0, :, half] = jnp.where(eighth == chunk, scale, scg[0, :, half])
            return inner

        lax.fori_loop(0, GU // 256, column_pair, 0)

        @pl.when(chunk + 2 < SHARD // 128)
        def _():
            for copy in gu_loads(chunk + 2):
                copy.start()

        return carry

    def adam_dn(chunk, carry):
        slot = chunk % 2
        for copy in dn_loads(chunk):
            copy.wait()
        rows = pl.ds(pl.multiple_of(chunk * 128, 128), 128)
        for n in range(HW // 256):
            cols = slice(n * 256, n * 256 + 256)
            fresh = adam(bm[slot, :, cols], bg[slot, :, cols], bf[slot, :, cols], bv[slot, :, cols])
            for h in range(2):
                block = 2 * n + h
                quant, scale = cast_block(fresh[:, h * 128 : h * 128 + 128])
                wdn[0, rows, block * 128 : block * 128 + 128] = quant
                scd[0, block : block + 1, rows] = jnp.broadcast_to(scale, (1, 128))

        @pl.when(chunk + 2 < SHARD // 128)
        def _():
            for copy in dn_loads(chunk + 2):
                copy.start()

        return carry

    def part_rows(p):
        return pl.ds(p * PART, PART)

    gu_sib, gu_far = [], []

    def send_gu(p):
        rows = part_rows(p)
        gu_far.append(
            start(remote(wgu.at[0, rows], wgu.at[2, rows], wg_s.at[1, p], wg_r.at[1, p], far_dev))
        )
        gu_sib.append(
            start(remote(wgu.at[0, rows], wgu.at[1, rows], wg_s.at[0, p], wg_r.at[0, p], sib_dev))
        )

    def build_maps():
        pk_copy.wait_recv()
        packed = pk[...]
        place = lax.broadcasted_iota(jnp.int32, (128, ROWS), 0)
        slot_no = lax.broadcasted_iota(jnp.int32, (128, ROWS), 1)
        lowest = (place - 64) * PAIR
        spread_slot = jnp.where((slot_no >= lowest) & (slot_no < lowest + PAIR), 1.0, 0.0).astype(BF16)
        low_weight = place * PAIR
        spread_weight = jnp.where(
            (slot_no >= low_weight) & (slot_no < low_weight + PAIR), 1.0, 0.0
        ).astype(BF16)
        t_row = lax.broadcasted_iota(jnp.int32, (2 * TOK, 2 * TOK), 0)
        t_col = lax.broadcasted_iota(jnp.int32, (2 * TOK, 2 * TOK), 1)
        same = (t_row >= TOK) == (t_col >= TOK)
        earlier = jnp.where((t_col < t_row) & same, 1.0, 0.0).astype(BF16)
        flags = packed.astype(BF16)
        counted = jnp.dot(earlier, flags, preferred_element_type=F32)
        token = lax.broadcasted_iota(jnp.int32, (2 * TOK, 128), 0)
        slot = counted + jnp.where(token >= TOK, float(CAP), 0.0)
        lanes = lax.broadcasted_iota(jnp.int32, (2 * TOK, 128), 1)
        chosen = (packed > 0.5) & (lanes >= 64)
        slot = jnp.where(chosen, slot, jnp.where(lanes >= 64, -1.0, 0.0)).astype(BF16)
        route = jnp.where(lanes < 64, packed, 0.0).astype(BF16)

        wide = lax.broadcasted_iota(jnp.int32, (1, ROWS), 1)
        within = wide
        for p in range(1, PLANE):
            within = within - jnp.where(wide >= p * PAIR, PAIR, 0)
        slots_wide = jnp.dot(slot, spread_slot, preferred_element_type=F32)
        route_wide = jnp.dot(route, spread_weight, preferred_element_type=F32)
        hit = slots_wide == within.astype(F32)
        comb[...] = jnp.where(hit, route_wide, 0.0).astype(BF16)
        sel[...] = jnp.transpose(jnp.where(hit, 1.0, 0.0)).astype(BF16)

    dispatched = [[] for _ in range(CHUNKS)]
    kept = []

    def dispatch(k):
        own_tok[k].wait()
        tok_copy[k].wait_recv()

        def column_tile(n, carry):
            cols = pl.ds(pl.multiple_of(n * 256, 256), 256)
            og[k, :, cols] = jnp.dot(
                sel[...], tokv[k, :, cols], preferred_element_type=F32
            ).astype(BF16)
            return carry

        lax.fori_loop(0, DC // 256, column_tile, 0)
        for i, (dev, p) in enumerate(peers):
            copy = remote(
                og.at[k, slot_rows(p)], xr.at[k, slot_rows(pe)], dis_s.at[k, i], dis_r.at[k, i], dev
            )
            copy.start()
            dispatched[k].append(copy)
        copy = pltpu.make_async_copy(og.at[k, slot_rows(pe)], xr.at[k, slot_rows(pe)], dis_l.at[k])
        copy.start()
        kept.append(copy)

    def arrived(k):
        kept[k].wait()
        for i, p in enumerate(sources):
            remote(
                og.at[k, slot_rows(p)],
                xr.at[k, slot_rows(p)],
                dis_s.at[k, i],
                dis_r.at[k, i],
                peers[i][0],
            ).wait_recv()

    lax.fori_loop(0, 2, adam_gu, 0)
    send_gu(0)
    build_maps()
    dispatch(0)
    lax.fori_loop(2, 4, adam_gu, 0)
    send_gu(1)
    dispatch(1)
    lax.fori_loop(4, 6, adam_gu, 0)
    send_gu(2)
    dispatch(2)
    lax.fori_loop(6, 8, adam_gu, 0)
    scg_far = start(remote(scg.at[0], scg.at[2], sc_s.at[1], sc_r.at[1], far_dev))
    scg_sib = start(remote(scg.at[0], scg.at[1], sc_s.at[0], sc_r.at[0], sib_dev))
    send_gu(3)
    dispatch(3)
    lax.fori_loop(0, 8, adam_dn, 0)
    scd_far = start(remote(scd.at[0], scd.at[2], sc_s.at[4], sc_r.at[4], far_dev))
    scd_sib = start(remote(scd.at[0], scd.at[1], sc_s.at[3], sc_r.at[3], sib_dev))
    dn_sib = start(remote(wdn.at[0], wdn.at[1], wd_s.at[0, 0], wd_r.at[0, 0], sib_dev))

    gu_fwd, dn_far, dn_fwd = [], [], []

    def forward_gu(p):
        gu_far[p].wait_recv()
        rows = part_rows(p)
        gu_fwd.append(
            start(remote(wgu.at[2, rows], wgu.at[3, rows], wg_s.at[2, p], wg_r.at[2, p], sib_dev))
        )

    def dn_rows(p):
        return pl.ds(p * 512, 512)

    def send_dn(p):
        rows = dn_rows(p)
        dn_far.append(
            start(remote(wdn.at[0, rows], wdn.at[2, rows], wd_s.at[1, p], wd_r.at[1, p], far_dev))
        )

    def forward_dn(p):
        dn_far[p].wait_recv()
        rows = dn_rows(p)
        dn_fwd.append(
            start(remote(wdn.at[2, rows], wdn.at[3, rows], wd_s.at[2, p], wd_r.at[2, p], sib_dev))
        )

    def gated(k, blocks, begin=False):
        def column_tile(n, carry):
            cols = pl.ds(pl.multiple_of(n * 256, 256), 256)
            total = None if begin else acc[:, cols]
            for b in blocks:
                inner = slice(b * 128, b * 128 + 128)
                piece = jnp.dot(
                    xr[k, :, inner], wgu[k, inner, cols], preferred_element_type=F32
                ) * scg[k, b : b + 1, cols]
                total = piece if total is None else total + piece
            acc[:, cols] = total
            return carry

        lax.fori_loop(0, GU // 256, column_tile, 0)

    arrived(0)
    gated(0, range(8), begin=True)
    forward_gu(0)
    scg_far.wait_recv()
    scg_fwd = start(remote(scg.at[2], scg.at[3], sc_s.at[2], sc_r.at[2], sib_dev))
    scg_sib.wait_recv()
    for p in range(PARTS):
        gu_sib[p].wait_recv()
    arrived(1)
    gated(1, range(8))
    forward_gu(1)
    arrived(2)
    gated(2, range(4))
    forward_gu(2)
    send_dn(0)
    gated(2, range(4, 6))
    arrived(3)
    scg_fwd.wait_recv()
    for p in range(3):
        gu_fwd[p].wait_recv()
    gated(3, range(6))
    forward_gu(3)
    send_dn(1)
    gated(2, range(6, 8))
    gu_fwd[3].wait_recv()
    gated(3, range(6, 8))

    def activate(n, carry):
        cols = pl.ds(pl.multiple_of(n * 256, 256), 256)
        gate = acc[:, cols]
        up = acc[:, pl.ds(pl.multiple_of(HW + n * 256, 256), 256)]
        hid[:, cols] = (gate / (1.0 + jnp.exp(-gate)) * up).astype(BF16)
        return carry

    lax.fori_loop(0, HW // 256, activate, 0)

    returned = []

    def lower(k):
        for copy in dispatched[k]:
            copy.wait_send()

        def row_tile(n, carry):
            cols = pl.ds(pl.multiple_of(n * 256, 256), 256)
            total = None
            for c in range(HW // 128):
                inner = slice(c * 128, c * 128 + 128)
                piece = lax.dot_general(
                    hid[:, inner],
                    wdn[k, cols, inner],
                    (((1,), (1,)), ((), ())),
                    preferred_element_type=F32,
                ) * scd[k, c : c + 1, cols]
                total = piece if total is None else total + piece
            og[k, :, cols] = total.astype(BF16)
            return carry

        lax.fori_loop(0, DC // 256, row_tile, 0)
        for i, (dev, p) in enumerate(peers):
            start(
                remote(
                    og.at[k, slot_rows(p)],
                    ret.at[k, slot_rows(pe)],
                    ret_s.at[k, i],
                    ret_r.at[k, i],
                    dev,
                )
            )
        copy = pltpu.make_async_copy(og.at[k, slot_rows(pe)], ret.at[k, slot_rows(pe)], ret_l.at[k])
        copy.start()
        returned.append(copy)

    partial = []

    def mix(k):
        returned[k].wait()
        for i, p in enumerate(sources):
            remote(
                og.at[k, slot_rows(p)],
                ret.at[k, slot_rows(p)],
                ret_s.at[k, i],
                ret_r.at[k, i],
                peers[i][0],
            ).wait_recv()

        def column_tile(n, carry):
            cols = pl.ds(pl.multiple_of(n * 256, 256), 256)
            both = jnp.dot(comb[...], ret[k, :, cols], preferred_element_type=F32)
            acc[k * TOK : (k + 1) * TOK, cols] = both[:TOK]
            ps[k, :, cols] = both[TOK:].astype(BF16)
            return carry

        lax.fori_loop(0, DC // 256, column_tile, 0)
        partial.append(start(remote(ps.at[k], pr.at[k], par_s.at[k], par_r.at[k], from_dev)))

    written = []
    apart = (y_to // 2 - yh) * (y_to // 2 - yh)

    def finish(k):
        partial[k].wait_recv()
        here = k + 2 * apart * (1 - 2 * (k // 2))
        rows = pl.ds(pl.multiple_of(here * TOK, TOK), TOK)
        tokv[k, 0:TOK, :] = (acc[rows, 0:DC] + pr[k].astype(F32)).astype(BF16)
        copy = pltpu.make_async_copy(
            tokv.at[k, pl.ds(0, TOK)], out.at[:, columns(zero_to, k)], out_sem.at[k]
        )
        copy.start()
        written.append(copy)

    lower(0)
    scd_sib.wait_recv()
    dn_sib.wait_recv()
    lower(1)
    scd_far.wait_recv()
    scd_fwd = start(remote(scd.at[2], scd.at[3], sc_s.at[5], sc_r.at[5], sib_dev))
    forward_dn(0)
    forward_dn(1)
    lower(2)
    scd_fwd.wait_recv()
    for p in range(2):
        dn_fwd[p].wait_recv()
    lower(3)
    mix(0)
    mix(1)
    mix(2)
    finish(0)
    mix(3)
    finish(2)
    finish(1)
    finish(3)
    for copy in sends:
        copy.wait_send()
    for copy in written:
        copy.wait()


def shards(*args):
    any_spec = pl.BlockSpec(memory_space=pl.ANY)
    vmem_spec = pl.BlockSpec(memory_space=pltpu.VMEM)
    dma = pltpu.SemaphoreType.DMA
    scratch = [
        pltpu.VMEM((CHUNKS, 2 * TOK, DC), BF16),
        pltpu.VMEM((2 * TOK, 128), F32),
        pltpu.VMEM((TOK, 128), F32),
        pltpu.VMEM((ROWS, 2 * TOK), BF16),
        pltpu.VMEM((2 * TOK, ROWS), BF16),
        pltpu.VMEM((CHUNKS, ROWS, DC), BF16),
        pltpu.VMEM((CHUNKS, ROWS, DC), BF16),
        pltpu.VMEM((4, SHARD, GU), BF16),
        pltpu.VMEM((4, SHARD, HW), BF16),
        pltpu.VMEM((4, 8, GU), F32),
        pltpu.VMEM((4, 8, SHARD), F32),
        pltpu.VMEM((ROWS, GU), F32),
        pltpu.VMEM((ROWS, HW), BF16),
        pltpu.VMEM((CHUNKS, ROWS, DC), BF16),
        pltpu.VMEM((CHUNKS, TOK, DC), BF16),
        pltpu.VMEM((CHUNKS, TOK, DC), BF16),
        pltpu.VMEM((2, 128, GU), F32),
        pltpu.VMEM((2, 128, GU), BF16),
        pltpu.VMEM((2, 128, GU), BF16),
        pltpu.VMEM((2, 128, GU), BF16),
        pltpu.VMEM((2, 128, HW), F32),
        pltpu.VMEM((2, 128, HW), BF16),
        pltpu.VMEM((2, 128, HW), BF16),
        pltpu.VMEM((2, 128, HW), BF16),
        dma((CHUNKS,)), dma((CHUNKS,)), dma((CHUNKS,)),
        dma, dma,
        dma((CHUNKS,)), dma((CHUNKS, PEERS)), dma((CHUNKS, PEERS)),
        dma((CHUNKS,)), dma((CHUNKS, PEERS)), dma((CHUNKS, PEERS)),
        dma((3, PARTS)), dma((3, PARTS)), dma((3, 2)), dma((3, 2)),
        dma((6,)), dma((6,)),
        dma((CHUNKS,)), dma((CHUNKS,)),
        dma((2, 4)), dma((2, 4)), dma((CHUNKS,)),
    ]
    return pl.pallas_call(
        kernel,
        name="layer",
        out_shape=jax.ShapeDtypeStruct((TOK, D), BF16),
        in_specs=[any_spec, vmem_spec, vmem_spec] + [any_spec] * 8,
        out_specs=any_spec,
        scratch_shapes=scratch,
        compiler_params=pltpu.CompilerParams(
            collective_id=0, has_side_effects=True, vmem_limit_bytes=60 * 1024 * 1024
        ),
        cost_estimate=pl.CostEstimate(
            flops=17_000_000_000, bytes_accessed=30_000_000, transcendentals=5_000_000
        ),
    )(*args)


def solution(mesh):
    rows = P(("expert", "zero"), None)
    weight = P("expert", "zero", None)
    in_specs = (rows,) * 3 + (weight,) * 8
    return jax.shard_map(shards, mesh=mesh, in_specs=in_specs, out_specs=rows, check_vma=False)
```

```python
import jax
import jax.numpy as jnp
from jax import lax
from jax.experimental import pallas as pl
from jax.experimental.pallas import tpu as pltpu
from jax.sharding import PartitionSpec as P

MESH = pl.DeviceIdType.MESH
F32 = jnp.float32
BF16 = jnp.bfloat16

TOK = 192
D = 4096
CAP = 24
PAIR = 2 * CAP
PLANE = 16
ROWS = PLANE * PAIR
GU = 1536
HW = 768
SHARD = 1024
CHUNKS = 4
DC = D // CHUNKS
PARTS = 4
PART = SHARD // PARTS

beta_one = 0.9
beta_two = 0.999
learn_rate = 0.002
adam_eps = 1e-08
corr_two = 0.63230457523

OFFSETS = (
    (2, 2), (1, 2), (3, 2), (2, 1), (2, 3), (1, 1), (3, 3), (1, 3), (3, 1),
    (2, 0), (0, 2), (1, 0), (3, 0), (0, 1), (0, 3),
)
PEERS = len(OFFSETS)


def remote(src, dst, send_sem, recv_sem, device):
    return pltpu.make_async_remote_copy(
        src_ref=src,
        dst_ref=dst,
        send_sem=send_sem,
        recv_sem=recv_sem,
        device_id=device,
        device_id_type=MESH,
    )


def chunk_of(zero, k):
    sibling = zero + 1 - 2 * (zero % 2)
    base = sibling if k % 2 else zero
    return (base + 2) % 4 if k >= 2 else base


def adam(master, grad, first, second):
    grads = grad.astype(F32)
    move = (learn_rate * beta_one) * first.astype(F32) + (learn_rate * (1.0 - beta_one)) * grads
    spread = (beta_two / corr_two) * second.astype(F32) + ((1.0 - beta_two) / corr_two) * grads * grads
    below = spread * lax.rsqrt(spread) + adam_eps
    inverse = pl.reciprocal(below, approx=True)
    inverse = inverse * (2.0 - below * inverse)
    return master - move * inverse


def fresh_chunk(master, grad, first, second, inv, slot, width, quant, put_scale):
    def update(r, best):
        rows = pl.ds(pl.multiple_of(r * 16, 16), 16)
        fresh = adam(master[slot, rows, :], grad[slot, rows, :], first[slot, rows, :], second[slot, rows, :])
        master[slot, rows, :] = fresh
        size = jnp.abs(fresh)
        return jnp.maximum(best, jnp.maximum(size[:8], size[8:]))

    best = lax.fori_loop(0, 8, update, jnp.zeros((8, width), F32))
    for b in range(width // 128):
        cols = slice(b * 128, b * 128 + 128)
        largest = jnp.max(jnp.max(best[:, cols], axis=0, keepdims=True), axis=1, keepdims=True)
        scale = ((largest + 1e-06) / 448.0).astype(BF16).astype(F32)
        put_scale(b, scale)
        inv[:, cols] = jnp.broadcast_to(1.0 / scale, (8, 128))

    def cast(r, carry):
        rows = pl.ds(pl.multiple_of(r * 16, 16), 16)
        quant(rows, (master[slot, rows, :] * inv[0:1, 0:width]).astype(BF16), r)
        return carry

    lax.fori_loop(0, 8, cast, 0)


def kernel(
    tokens, ids, weights,
    mgu, ggu, fgu, vgu, mdn, gdn, fdn, vdn,
    out,
    tokv, pk, pks, sel, comb, og, xr, wgu, wdn, scg, scd, acc, hid, ret, ps, pr,
    am, ag, af, av, bm, bg, bf, bv, inv,
    tok_l, tok_s, tok_r, pk_s, pk_r, dis_l, dis_s, dis_r, ret_l, ret_s, ret_r,
    wg_s, wg_r, wd_s, wd_r, sc_s, sc_r, par_s, par_r, a_sem, b_sem, out_sem,
):
    expert = lax.axis_index("expert")
    zero = lax.axis_index("zero")
    x, zz, yl = expert // 8, (expert // 2) % 4, expert % 2
    yh, core = zero // 2, zero % 2
    y = yh * 2 + yl
    pe = x * 4 + zz
    step = 1 - 2 * core

    def at(px, py, pz, pc):
        return (px * 8 + pz * 2 + py % 2, (py // 2) * 2 + pc)

    y_to, y_from = (y + step + 4) % 4, (y - step + 4) % 4
    to_dev = at(x, y_to, zz, core)
    from_dev = at(x, y_from, zz, core)
    sib_dev = at(x, y, zz, 1 - core)
    far_dev = at(x, (y + 2) % 4, zz, core)
    zero_to = (y_to // 2) * 2 + core

    peers = []
    sources = []
    for dx, dz in OFFSETS:
        px, pz = (x + dx) % 4, (zz + dz) % 4
        qx, qz = (x + 4 - dx) % 4, (zz + 4 - dz) % 4
        peers.append((at(px, y, pz, core), px * 4 + pz))
        sources.append(qx * 4 + qz)

    def slot_rows(p):
        return pl.ds(pl.multiple_of(p * PAIR, 16), PAIR)

    def columns(zero_index, k):
        return pl.ds(pl.multiple_of(chunk_of(zero_index, k) * DC, DC), DC)

    own_tok = []
    for k in range(CHUNKS):
        copy = pltpu.make_async_copy(
            tokens.at[:, columns(zero, k)], tokv.at[k, pl.ds(0, TOK)], tok_l.at[k]
        )
        copy.start()
        own_tok.append(copy)

    def gu_loads(chunk):
        slot = chunk % 2
        rows = pl.ds(pl.multiple_of(chunk * 128, 128), 128)
        return [
            pltpu.make_async_copy(src.at[0, rows], dst.at[slot], a_sem.at[slot, i])
            for i, (src, dst) in enumerate(((mgu, am), (ggu, ag), (fgu, af), (vgu, av)))
        ]

    def dn_loads(chunk):
        slot = chunk % 2
        rows = pl.ds(pl.multiple_of(chunk * 128, 128), 128)
        return [
            pltpu.make_async_copy(src.at[0, rows], dst.at[slot], b_sem.at[slot, i])
            for i, (src, dst) in enumerate(((mdn, bm), (gdn, bg), (fdn, bf), (vdn, bv)))
        ]

    for chunk in range(2):
        for copy in gu_loads(chunk):
            copy.start()
    for chunk in range(2):
        for copy in dn_loads(chunk):
            copy.start()

    lane = lax.broadcasted_iota(jnp.int32, (TOK, 128), 1)
    mine = jnp.zeros((TOK, 128), F32)
    theirs = jnp.zeros((TOK, 128), F32)
    for k in range(8):
        named = ids[:, k : k + 1]
        weight = weights[:, k : k + 1].astype(F32)
        for other in range(2):
            row = yl if other == 0 else 1 - yl
            value = jnp.where(
                named == lane * 8 + 4 * row,
                weight,
                jnp.where(named == (lane - 64) * 8 + 4 * row, 1.0, 0.0),
            )
            if other == 0:
                mine = mine + value
            else:
                theirs = theirs + value
    pk[0:TOK, :] = mine
    pks[...] = theirs

    barrier = pltpu.get_barrier_semaphore()
    greeted = [dev for dev, _ in peers] + [sib_dev, far_dev, to_dev, from_dev]
    for dev in greeted:
        pl.semaphore_signal(barrier, inc=1, device_id=dev, device_id_type=MESH)
    pl.semaphore_wait(barrier, len(greeted))

    sends = []

    def start(copy):
        copy.start()
        sends.append(copy)
        return copy

    apart = (y_to // 2 - yh) * (y_to // 2 - yh)
    for k in range(CHUNKS):
        own_tok[k].wait()
    pk_copy = start(remote(pks, pk.at[pl.ds(TOK, TOK)], pk_s, pk_r, to_dev))
    tok_copy = [
        remote(
                tokv.at[k + 2 * apart * (1 - 2 * (k // 2)), pl.ds(0, TOK)],
                tokv.at[k, pl.ds(TOK, TOK)],
                tok_s.at[k],
                tok_r.at[k],
                to_dev,
        )
        for k in range(CHUNKS)
    ]
    for copy in tok_copy:
        copy.start()

    eighth = lax.broadcasted_iota(jnp.int32, (8, 128), 0)
    scg[0] = jnp.zeros((8, GU), F32)
    scd[0] = jnp.zeros((8, SHARD), F32)

    def adam_gu(chunk, carry):
        for copy in gu_loads(chunk):
            copy.wait()

        def quant(rows, value, r):
            wgu[0, pl.ds(pl.multiple_of(chunk * 128 + r * 16, 16), 16), :] = value

        def put_scale(b, scale):
            cols = slice(b * 128, b * 128 + 128)
            scg[0, :, cols] = jnp.where(eighth == chunk, scale, scg[0, :, cols])

        fresh_chunk(am, ag, af, av, inv, chunk % 2, GU, quant, put_scale)

        @pl.when(chunk + 2 < SHARD // 128)
        def _():
            for copy in gu_loads(chunk + 2):
                copy.start()

        return carry

    def adam_dn(chunk, carry):
        for copy in dn_loads(chunk):
            copy.wait()
        cols = pl.ds(pl.multiple_of(chunk * 128, 128), 128)

        def quant(rows, value, r):
            wdn[0, pl.ds(pl.multiple_of(chunk * 128 + r * 16, 16), 16), :] = value

        def put_scale(b, scale):
            scd[0, b : b + 1, cols] = jnp.broadcast_to(scale, (1, 128))

        fresh_chunk(bm, bg, bf, bv, inv, chunk % 2, HW, quant, put_scale)

        @pl.when(chunk + 2 < SHARD // 128)
        def _():
            for copy in dn_loads(chunk + 2):
                copy.start()

        return carry

    def part_rows(p):
        return pl.ds(p * PART, PART)

    gu_sib, gu_far = [], []

    def send_gu(p):
        rows = part_rows(p)
        gu_far.append(
            start(remote(wgu.at[0, rows], wgu.at[2, rows], wg_s.at[1, p], wg_r.at[1, p], far_dev))
        )
        gu_sib.append(
            start(remote(wgu.at[0, rows], wgu.at[1, rows], wg_s.at[0, p], wg_r.at[0, p], sib_dev))
        )

    def build_maps():
        pk_copy.wait_recv()
        packed = pk[...]
        place = lax.broadcasted_iota(jnp.int32, (128, ROWS), 0)
        slot_no = lax.broadcasted_iota(jnp.int32, (128, ROWS), 1)
        lowest = (place - 64) * PAIR
        spread_slot = jnp.where((slot_no >= lowest) & (slot_no < lowest + PAIR), 1.0, 0.0).astype(BF16)
        low_weight = place * PAIR
        spread_weight = jnp.where(
            (slot_no >= low_weight) & (slot_no < low_weight + PAIR), 1.0, 0.0
        ).astype(BF16)
        t_row = lax.broadcasted_iota(jnp.int32, (2 * TOK, 2 * TOK), 0)
        t_col = lax.broadcasted_iota(jnp.int32, (2 * TOK, 2 * TOK), 1)
        same = (t_row >= TOK) == (t_col >= TOK)
        earlier = jnp.where((t_col < t_row) & same, 1.0, 0.0).astype(BF16)
        flags = packed.astype(BF16)
        counted = jnp.dot(earlier, flags, preferred_element_type=F32)
        token = lax.broadcasted_iota(jnp.int32, (2 * TOK, 128), 0)
        slot = counted + jnp.where(token >= TOK, float(CAP), 0.0)
        lanes = lax.broadcasted_iota(jnp.int32, (2 * TOK, 128), 1)
        chosen = (packed > 0.5) & (lanes >= 64)
        slot = jnp.where(chosen, slot, jnp.where(lanes >= 64, -1.0, 0.0)).astype(BF16)
        route = jnp.where(lanes < 64, packed, 0.0).astype(BF16)

        wide = lax.broadcasted_iota(jnp.int32, (1, ROWS), 1)
        within = wide
        for p in range(1, PLANE):
            within = within - jnp.where(wide >= p * PAIR, PAIR, 0)
        slots_wide = jnp.dot(slot, spread_slot, preferred_element_type=F32)
        route_wide = jnp.dot(route, spread_weight, preferred_element_type=F32)
        hit = slots_wide == within.astype(F32)
        comb[...] = jnp.where(hit, route_wide, 0.0).astype(BF16)
        sel[...] = jnp.transpose(jnp.where(hit, 1.0, 0.0)).astype(BF16)

    dispatched = [[] for _ in range(CHUNKS)]
    kept = []

    def dispatch(k):
        tok_copy[k].wait_recv()

        def column_tile(n, carry):
            cols = pl.ds(pl.multiple_of(n * 256, 256), 256)
            og[k, :, cols] = jnp.dot(
                sel[...], tokv[k, :, cols], preferred_element_type=F32
            ).astype(BF16)
            return carry

        lax.fori_loop(0, DC // 256, column_tile, 0)
        for i, (dev, p) in enumerate(peers):
            copy = remote(
                og.at[k, slot_rows(p)], xr.at[k, slot_rows(pe)], dis_s.at[k, i], dis_r.at[k, i], dev
            )
            copy.start()
            dispatched[k].append(copy)
        copy = pltpu.make_async_copy(og.at[k, slot_rows(pe)], xr.at[k, slot_rows(pe)], dis_l.at[k])
        copy.start()
        kept.append(copy)

    def arrived(k):
        kept[k].wait()
        for i, p in enumerate(sources):
            remote(
                og.at[k, slot_rows(p)],
                xr.at[k, slot_rows(p)],
                dis_s.at[k, i],
                dis_r.at[k, i],
                peers[i][0],
            ).wait_recv()

    lax.fori_loop(0, 2, adam_gu, 0)
    build_maps()
    dispatch(0)
    lax.fori_loop(2, 4, adam_gu, 0)
    dispatch(1)
    lax.fori_loop(4, 6, adam_gu, 0)
    dispatch(2)
    lax.fori_loop(6, 8, adam_gu, 0)
    dispatch(3)
    scg_far = start(remote(scg.at[0], scg.at[2], sc_s.at[1], sc_r.at[1], far_dev))
    scg_sib = start(remote(scg.at[0], scg.at[1], sc_s.at[0], sc_r.at[0], sib_dev))
    send_gu(0)
    send_gu(1)
    send_gu(2)
    send_gu(3)
    lax.fori_loop(0, 8, adam_dn, 0)
    scd_far = start(remote(scd.at[0], scd.at[2], sc_s.at[4], sc_r.at[4], far_dev))
    scd_sib = start(remote(scd.at[0], scd.at[1], sc_s.at[3], sc_r.at[3], sib_dev))
    dn_sib = start(remote(wdn.at[0], wdn.at[1], wd_s.at[0, 0], wd_r.at[0, 0], sib_dev))

    gu_fwd, dn_far, dn_fwd = [], [], []

    def forward_gu(p):
        gu_far[p].wait_recv()
        rows = part_rows(p)
        gu_fwd.append(
            start(remote(wgu.at[2, rows], wgu.at[3, rows], wg_s.at[2, p], wg_r.at[2, p], sib_dev))
        )

    def dn_rows(p):
        return pl.ds(p * 512, 512)

    def send_dn(p):
        rows = dn_rows(p)
        dn_far.append(
            start(remote(wdn.at[0, rows], wdn.at[2, rows], wd_s.at[1, p], wd_r.at[1, p], far_dev))
        )

    def forward_dn(p):
        dn_far[p].wait_recv()
        rows = dn_rows(p)
        dn_fwd.append(
            start(remote(wdn.at[2, rows], wdn.at[3, rows], wd_s.at[2, p], wd_r.at[2, p], sib_dev))
        )

    def gated(k, blocks, begin=False):
        def column_tile(n, carry):
            cols = pl.ds(pl.multiple_of(n * 256, 256), 256)
            total = None if begin else acc[:, cols]
            for b in blocks:
                inner = slice(b * 128, b * 128 + 128)
                piece = jnp.dot(
                    xr[k, :, inner], wgu[k, inner, cols], preferred_element_type=F32
                ) * scg[k, b : b + 1, cols]
                total = piece if total is None else total + piece
            acc[:, cols] = total
            return carry

        lax.fori_loop(0, GU // 256, column_tile, 0)

    arrived(0)
    gated(0, range(8), begin=True)
    forward_gu(0)
    scg_far.wait_recv()
    scg_fwd = start(remote(scg.at[2], scg.at[3], sc_s.at[2], sc_r.at[2], sib_dev))
    scg_sib.wait_recv()
    for p in range(PARTS):
        gu_sib[p].wait_recv()
    arrived(1)
    gated(1, range(8))
    forward_gu(1)
    arrived(2)
    gated(2, range(4))
    forward_gu(2)
    send_dn(0)
    gated(2, range(4, 6))
    arrived(3)
    scg_fwd.wait_recv()
    for p in range(3):
        gu_fwd[p].wait_recv()
    gated(3, range(6))
    forward_gu(3)
    send_dn(1)
    gated(2, range(6, 8))
    gu_fwd[3].wait_recv()
    gated(3, range(6, 8))

    def activate(n, carry):
        cols = pl.ds(pl.multiple_of(n * 256, 256), 256)
        gate = acc[:, cols]
        up = acc[:, pl.ds(pl.multiple_of(HW + n * 256, 256), 256)]
        hid[:, cols] = (gate / (1.0 + jnp.exp(-gate)) * up).astype(BF16)
        return carry

    lax.fori_loop(0, HW // 256, activate, 0)

    returned = []

    def lower(k):
        for copy in dispatched[k]:
            copy.wait_send()

        def row_tile(n, carry):
            cols = pl.ds(pl.multiple_of(n * 256, 256), 256)
            total = None
            for c in range(HW // 128):
                inner = slice(c * 128, c * 128 + 128)
                piece = lax.dot_general(
                    hid[:, inner],
                    wdn[k, cols, inner],
                    (((1,), (1,)), ((), ())),
                    preferred_element_type=F32,
                ) * scd[k, c : c + 1, cols]
                total = piece if total is None else total + piece
            og[k, :, cols] = total.astype(BF16)
            return carry

        lax.fori_loop(0, DC // 256, row_tile, 0)
        for i, (dev, p) in enumerate(peers):
            start(
                remote(
                    og.at[k, slot_rows(p)],
                    ret.at[k, slot_rows(pe)],
                    ret_s.at[k, i],
                    ret_r.at[k, i],
                    dev,
                )
            )
        copy = pltpu.make_async_copy(og.at[k, slot_rows(pe)], ret.at[k, slot_rows(pe)], ret_l.at[k])
        copy.start()
        returned.append(copy)

    partial = []

    def mix(k):
        returned[k].wait()
        for i, p in enumerate(sources):
            remote(
                og.at[k, slot_rows(p)],
                ret.at[k, slot_rows(p)],
                ret_s.at[k, i],
                ret_r.at[k, i],
                peers[i][0],
            ).wait_recv()

        def column_tile(n, carry):
            cols = pl.ds(pl.multiple_of(n * 256, 256), 256)
            both = jnp.dot(comb[...], ret[k, :, cols], preferred_element_type=F32)
            acc[k * TOK : (k + 1) * TOK, cols] = both[:TOK]
            ps[k, :, cols] = both[TOK:].astype(BF16)
            return carry

        lax.fori_loop(0, DC // 256, column_tile, 0)
        partial.append(start(remote(ps.at[k], pr.at[k], par_s.at[k], par_r.at[k], from_dev)))

    written = []

    def finish(k):
        partial[k].wait_recv()
        here = k + 2 * apart * (1 - 2 * (k // 2))
        rows = pl.ds(pl.multiple_of(here * TOK, TOK), TOK)
        tokv[k, 0:TOK, :] = (acc[rows, 0:DC] + pr[k].astype(F32)).astype(BF16)
        copy = pltpu.make_async_copy(
            tokv.at[k, pl.ds(0, TOK)], out.at[:, columns(zero_to, k)], out_sem.at[k]
        )
        copy.start()
        written.append(copy)

    for copy in tok_copy:
        copy.wait_send()
    lower(0)
    scd_sib.wait_recv()
    dn_sib.wait_recv()
    lower(1)
    scd_far.wait_recv()
    scd_fwd = start(remote(scd.at[2], scd.at[3], sc_s.at[5], sc_r.at[5], sib_dev))
    forward_dn(0)
    forward_dn(1)
    lower(2)
    scd_fwd.wait_recv()
    for p in range(2):
        dn_fwd[p].wait_recv()
    lower(3)
    mix(0)
    mix(1)
    mix(2)
    finish(0)
    mix(3)
    finish(2)
    finish(1)
    finish(3)
    for copy in sends:
        copy.wait_send()
    for copy in written:
        copy.wait()


def shards(*args):
    any_spec = pl.BlockSpec(memory_space=pl.ANY)
    vmem_spec = pl.BlockSpec(memory_space=pltpu.VMEM)
    dma = pltpu.SemaphoreType.DMA
    scratch = [
        pltpu.VMEM((CHUNKS, 2 * TOK, DC), BF16),
        pltpu.VMEM((2 * TOK, 128), F32),
        pltpu.VMEM((TOK, 128), F32),
        pltpu.VMEM((ROWS, 2 * TOK), BF16),
        pltpu.VMEM((2 * TOK, ROWS), BF16),
        pltpu.VMEM((CHUNKS, ROWS, DC), BF16),
        pltpu.VMEM((CHUNKS, ROWS, DC), BF16),
        pltpu.VMEM((4, SHARD, GU), BF16),
        pltpu.VMEM((4, SHARD, HW), BF16),
        pltpu.VMEM((4, 8, GU), F32),
        pltpu.VMEM((4, 8, SHARD), F32),
        pltpu.VMEM((ROWS, GU), F32),
        pltpu.VMEM((ROWS, HW), BF16),
        pltpu.VMEM((CHUNKS, ROWS, DC), BF16),
        pltpu.VMEM((CHUNKS, TOK, DC), BF16),
        pltpu.VMEM((CHUNKS, TOK, DC), BF16),
        pltpu.VMEM((2, 128, GU), F32),
        pltpu.VMEM((2, 128, GU), BF16),
        pltpu.VMEM((2, 128, GU), BF16),
        pltpu.VMEM((2, 128, GU), BF16),
        pltpu.VMEM((2, 128, HW), F32),
        pltpu.VMEM((2, 128, HW), BF16),
        pltpu.VMEM((2, 128, HW), BF16),
        pltpu.VMEM((2, 128, HW), BF16),
        pltpu.VMEM((8, GU), F32),
        dma((CHUNKS,)), dma((CHUNKS,)), dma((CHUNKS,)),
        dma, dma,
        dma((CHUNKS,)), dma((CHUNKS, PEERS)), dma((CHUNKS, PEERS)),
        dma((CHUNKS,)), dma((CHUNKS, PEERS)), dma((CHUNKS, PEERS)),
        dma((3, PARTS)), dma((3, PARTS)), dma((3, 2)), dma((3, 2)),
        dma((6,)), dma((6,)),
        dma((CHUNKS,)), dma((CHUNKS,)),
        dma((2, 4)), dma((2, 4)), dma((CHUNKS,)),
    ]
    return pl.pallas_call(
        kernel,
        name="layer",
        out_shape=jax.ShapeDtypeStruct((TOK, D), BF16),
        in_specs=[any_spec, vmem_spec, vmem_spec] + [any_spec] * 8,
        out_specs=any_spec,
        scratch_shapes=scratch,
        compiler_params=pltpu.CompilerParams(
            collective_id=0, has_side_effects=True, vmem_limit_bytes=60 * 1024 * 1024
        ),
        cost_estimate=pl.CostEstimate(
            flops=17_000_000_000, bytes_accessed=30_000_000, transcendentals=5_000_000
        ),
    )(*args)


def solution(mesh):
    rows = P(("expert", "zero"), None)
    weight = P("expert", "zero", None)
    in_specs = (rows,) * 3 + (weight,) * 8
    return jax.shard_map(shards, mesh=mesh, in_specs=in_specs, out_specs=rows, check_vma=False)
```

```python
import jax
import jax.numpy as jnp
from jax import lax
from jax.experimental import pallas as pl
from jax.experimental.pallas import tpu as pltpu
from jax.sharding import PartitionSpec as P

MESH = pl.DeviceIdType.MESH
F32 = jnp.float32
BF16 = jnp.bfloat16

TOK = 192
D = 4096
CAP = 24
PAIR = 2 * CAP
PLANE = 16
ROWS = PLANE * PAIR
GU = 1536
HW = 768
SHARD = 1024
CHUNKS = 4
DC = D // CHUNKS
PARTS = 4
PART = SHARD // PARTS

beta_one = 0.9
beta_two = 0.999
learn_rate = 0.002
adam_eps = 1e-08
corr_two = 0.63230457523

OFFSETS = (
    (2, 2), (1, 2), (3, 2), (2, 1), (2, 3), (1, 1), (3, 3), (1, 3), (3, 1),
    (2, 0), (0, 2), (1, 0), (3, 0), (0, 1), (0, 3),
)
PEERS = len(OFFSETS)


def remote(src, dst, send_sem, recv_sem, device):
    return pltpu.make_async_remote_copy(
        src_ref=src,
        dst_ref=dst,
        send_sem=send_sem,
        recv_sem=recv_sem,
        device_id=device,
        device_id_type=MESH,
    )


def chunk_of(zero, k):
    sibling = zero + 1 - 2 * (zero % 2)
    base = sibling if k % 2 else zero
    return (base + 2) % 4 if k >= 2 else base


def adam(master, grad, first, second):
    grads = grad.astype(F32)
    move = (learn_rate * beta_one) * first.astype(F32) + (learn_rate * (1.0 - beta_one)) * grads
    spread = (beta_two / corr_two) * second.astype(F32) + ((1.0 - beta_two) / corr_two) * grads * grads
    below = spread * lax.rsqrt(spread) + adam_eps
    inverse = pl.reciprocal(below, approx=True)
    inverse = inverse * (2.0 - below * inverse)
    return master - move * inverse


def fresh_chunk(master, grad, first, second, inv, slot, width, quant, put_scale):
    def update(r, best):
        rows = pl.ds(pl.multiple_of(r * 16, 16), 16)
        fresh = adam(master[slot, rows, :], grad[slot, rows, :], first[slot, rows, :], second[slot, rows, :])
        master[slot, rows, :] = fresh
        size = jnp.abs(fresh)
        return jnp.maximum(best, jnp.maximum(size[:8], size[8:]))

    best = lax.fori_loop(0, 8, update, jnp.zeros((8, width), F32))
    for b in range(width // 128):
        cols = slice(b * 128, b * 128 + 128)
        largest = jnp.max(jnp.max(best[:, cols], axis=0, keepdims=True), axis=1, keepdims=True)
        scale = ((largest + 1e-06) / 448.0).astype(BF16).astype(F32)
        put_scale(b, scale)
        inv[:, cols] = jnp.broadcast_to(1.0 / scale, (8, 128))

    def cast(r, carry):
        rows = pl.ds(pl.multiple_of(r * 16, 16), 16)
        quant(rows, (master[slot, rows, :] * inv[0:1, 0:width]).astype(BF16), r)
        return carry

    lax.fori_loop(0, 8, cast, 0)


def kernel(
    tokens, ids, weights,
    mgu, ggu, fgu, vgu, mdn, gdn, fdn, vdn,
    out,
    tokv, pk, pks, sel, comb, og, xr, wgu, wdn, scg, scd, acc, hid, ret, ps, pr,
    am, ag, af, av, bm, bg, bf, bv, inv,
    tok_l, tok_s, tok_r, pk_s, pk_r, dis_l, dis_s, dis_r, ret_l, ret_s, ret_r,
    wg_s, wg_r, wd_s, wd_r, sc_s, sc_r, par_s, par_r, a_sem, b_sem, out_sem,
):
    expert = lax.axis_index("expert")
    zero = lax.axis_index("zero")
    x, zz, yl = expert // 8, (expert // 2) % 4, expert % 2
    yh, core = zero // 2, zero % 2
    y = yh * 2 + yl
    pe = x * 4 + zz
    step = 1 - 2 * core

    def at(px, py, pz, pc):
        return (px * 8 + pz * 2 + py % 2, (py // 2) * 2 + pc)

    y_to, y_from = (y + step + 4) % 4, (y - step + 4) % 4
    to_dev = at(x, y_to, zz, core)
    from_dev = at(x, y_from, zz, core)
    sib_dev = at(x, y, zz, 1 - core)
    far_dev = at(x, (y + 2) % 4, zz, core)
    zero_to = (y_to // 2) * 2 + core

    peers = []
    sources = []
    for ax, az in OFFSETS:
        dx, dz = ax + (az - ax) * core, az + (ax - az) * core
        px, pz = (x + dx) % 4, (zz + dz) % 4
        qx, qz = (x + 4 - dx) % 4, (zz + 4 - dz) % 4
        peers.append((at(px, y, pz, core), px * 4 + pz))
        sources.append(qx * 4 + qz)

    def slot_rows(p):
        return pl.ds(pl.multiple_of(p * PAIR, 16), PAIR)

    def columns(zero_index, k):
        return pl.ds(pl.multiple_of(chunk_of(zero_index, k) * DC, DC), DC)

    own_tok = []
    for k in range(CHUNKS):
        copy = pltpu.make_async_copy(
            tokens.at[:, columns(zero, k)], tokv.at[k, pl.ds(0, TOK)], tok_l.at[k]
        )
        copy.start()
        own_tok.append(copy)

    def gu_loads(chunk):
        slot = chunk % 2
        rows = pl.ds(pl.multiple_of(chunk * 128, 128), 128)
        return [
            pltpu.make_async_copy(src.at[0, rows], dst.at[slot], a_sem.at[slot, i])
            for i, (src, dst) in enumerate(((mgu, am), (ggu, ag), (fgu, af), (vgu, av)))
        ]

    def dn_loads(chunk):
        slot = chunk % 2
        rows = pl.ds(pl.multiple_of(chunk * 128, 128), 128)
        return [
            pltpu.make_async_copy(src.at[0, rows], dst.at[slot], b_sem.at[slot, i])
            for i, (src, dst) in enumerate(((mdn, bm), (gdn, bg), (fdn, bf), (vdn, bv)))
        ]

    for chunk in range(2):
        for copy in gu_loads(chunk):
            copy.start()
    for chunk in range(2):
        for copy in dn_loads(chunk):
            copy.start()

    lane = lax.broadcasted_iota(jnp.int32, (128, TOK), 0)
    mine = jnp.zeros((128, TOK), F32)
    theirs = jnp.zeros((128, TOK), F32)
    for k in range(8):
        named = ids[k : k + 1, :]
        weight = weights[k : k + 1, :].astype(F32)
        for other in range(2):
            row = yl if other == 0 else 1 - yl
            value = jnp.where(
                named == lane * 8 + 4 * row,
                weight,
                jnp.where(named == (lane - 64) * 8 + 4 * row, 1.0, 0.0),
            )
            if other == 0:
                mine = mine + value
            else:
                theirs = theirs + value
    pk[0:TOK, :] = jnp.transpose(mine)
    pks[...] = jnp.transpose(theirs)

    barrier = pltpu.get_barrier_semaphore()
    greeted = [dev for dev, _ in peers] + [sib_dev, far_dev, to_dev, from_dev]
    for dev in greeted:
        pl.semaphore_signal(barrier, inc=1, device_id=dev, device_id_type=MESH)
    pl.semaphore_wait(barrier, len(greeted))

    sends = []

    def start(copy):
        copy.start()
        sends.append(copy)
        return copy

    apart = (y_to // 2 - yh) * (y_to // 2 - yh)
    for k in range(CHUNKS):
        own_tok[k].wait()
    pk_copy = start(remote(pks, pk.at[pl.ds(TOK, TOK)], pk_s, pk_r, to_dev))
    tok_copy = [
        remote(
                tokv.at[k + 2 * apart * (1 - 2 * (k // 2)), pl.ds(0, TOK)],
                tokv.at[k, pl.ds(TOK, TOK)],
                tok_s.at[k],
                tok_r.at[k],
                to_dev,
        )
        for k in range(CHUNKS)
    ]
    for copy in tok_copy:
        copy.start()

    eighth = lax.broadcasted_iota(jnp.int32, (8, 128), 0)
    scg[0] = jnp.zeros((8, GU), F32)
    scd[0] = jnp.zeros((8, SHARD), F32)

    def adam_gu(chunk, carry):
        for copy in gu_loads(chunk):
            copy.wait()

        def quant(rows, value, r):
            wgu[0, pl.ds(pl.multiple_of(chunk * 128 + r * 16, 16), 16), :] = value

        def put_scale(b, scale):
            cols = slice(b * 128, b * 128 + 128)
            scg[0, :, cols] = jnp.where(eighth == chunk, scale, scg[0, :, cols])

        fresh_chunk(am, ag, af, av, inv, chunk % 2, GU, quant, put_scale)

        @pl.when(chunk + 2 < SHARD // 128)
        def _():
            for copy in gu_loads(chunk + 2):
                copy.start()

        return carry

    def adam_dn(chunk, carry):
        for copy in dn_loads(chunk):
            copy.wait()
        cols = pl.ds(pl.multiple_of(chunk * 128, 128), 128)

        def quant(rows, value, r):
            wdn[0, pl.ds(pl.multiple_of(chunk * 128 + r * 16, 16), 16), :] = value

        def put_scale(b, scale):
            scd[0, b : b + 1, cols] = jnp.broadcast_to(scale, (1, 128))

        fresh_chunk(bm, bg, bf, bv, inv, chunk % 2, HW, quant, put_scale)

        @pl.when(chunk + 2 < SHARD // 128)
        def _():
            for copy in dn_loads(chunk + 2):
                copy.start()

        return carry

    def part_rows(p):
        return pl.ds(p * PART, PART)

    gu_sib, gu_far = [], []

    def send_gu(p):
        rows = part_rows(p)
        gu_far.append(
            start(remote(wgu.at[0, rows], wgu.at[2, rows], wg_s.at[1, p], wg_r.at[1, p], far_dev))
        )
        gu_sib.append(
            start(remote(wgu.at[0, rows], wgu.at[1, rows], wg_s.at[0, p], wg_r.at[0, p], sib_dev))
        )

    def build_maps():
        pk_copy.wait_recv()
        packed = pk[...]
        place = lax.broadcasted_iota(jnp.int32, (128, ROWS), 0)
        slot_no = lax.broadcasted_iota(jnp.int32, (128, ROWS), 1)
        lowest = (place - 64) * PAIR
        spread_slot = jnp.where((slot_no >= lowest) & (slot_no < lowest + PAIR), 1.0, 0.0).astype(BF16)
        low_weight = place * PAIR
        spread_weight = jnp.where(
            (slot_no >= low_weight) & (slot_no < low_weight + PAIR), 1.0, 0.0
        ).astype(BF16)
        t_row = lax.broadcasted_iota(jnp.int32, (2 * TOK, 2 * TOK), 0)
        t_col = lax.broadcasted_iota(jnp.int32, (2 * TOK, 2 * TOK), 1)
        same = (t_row >= TOK) == (t_col >= TOK)
        earlier = jnp.where((t_col < t_row) & same, 1.0, 0.0).astype(BF16)
        flags = packed.astype(BF16)
        counted = jnp.dot(earlier, flags, preferred_element_type=F32)
        token = lax.broadcasted_iota(jnp.int32, (2 * TOK, 128), 0)
        slot = counted + jnp.where(token >= TOK, float(CAP), 0.0)
        lanes = lax.broadcasted_iota(jnp.int32, (2 * TOK, 128), 1)
        chosen = (packed > 0.5) & (lanes >= 64)
        slot = jnp.where(chosen, slot, jnp.where(lanes >= 64, -1.0, 0.0)).astype(BF16)
        route = jnp.where(lanes < 64, packed, 0.0).astype(BF16)

        wide = lax.broadcasted_iota(jnp.int32, (1, ROWS), 1)
        within = wide
        for p in range(1, PLANE):
            within = within - jnp.where(wide >= p * PAIR, PAIR, 0)
        slots_wide = jnp.dot(slot, spread_slot, preferred_element_type=F32)
        route_wide = jnp.dot(route, spread_weight, preferred_element_type=F32)
        hit = slots_wide == within.astype(F32)
        comb[...] = jnp.where(hit, route_wide, 0.0).astype(BF16)
        sel[...] = jnp.transpose(jnp.where(hit, 1.0, 0.0)).astype(BF16)

    dispatched = [[] for _ in range(CHUNKS)]
    kept = []

    def dispatch(k):
        tok_copy[k].wait_recv()

        def column_tile(n, carry):
            cols = pl.ds(pl.multiple_of(n * 256, 256), 256)
            og[k, :, cols] = jnp.dot(
                sel[...], tokv[k, :, cols], preferred_element_type=F32
            ).astype(BF16)
            return carry

        lax.fori_loop(0, DC // 256, column_tile, 0)
        for i, (dev, p) in enumerate(peers):
            copy = remote(
                og.at[k, slot_rows(p)], xr.at[k, slot_rows(pe)], dis_s.at[k, i], dis_r.at[k, i], dev
            )
            copy.start()
            dispatched[k].append(copy)
        copy = pltpu.make_async_copy(og.at[k, slot_rows(pe)], xr.at[k, slot_rows(pe)], dis_l.at[k])
        copy.start()
        kept.append(copy)

    def arrived(k):
        kept[k].wait()
        for i, p in enumerate(sources):
            remote(
                og.at[k, slot_rows(p)],
                xr.at[k, slot_rows(p)],
                dis_s.at[k, i],
                dis_r.at[k, i],
                peers[i][0],
            ).wait_recv()

    lax.fori_loop(0, 2, adam_gu, 0)
    build_maps()
    dispatch(0)
    lax.fori_loop(2, 4, adam_gu, 0)
    dispatch(1)
    lax.fori_loop(4, 6, adam_gu, 0)
    dispatch(2)
    lax.fori_loop(6, 8, adam_gu, 0)
    send_gu(0)
    dispatch(3)
    scg_far = start(remote(scg.at[0], scg.at[2], sc_s.at[1], sc_r.at[1], far_dev))
    scg_sib = start(remote(scg.at[0], scg.at[1], sc_s.at[0], sc_r.at[0], sib_dev))
    send_gu(1)
    send_gu(2)
    send_gu(3)
    lax.fori_loop(0, 8, adam_dn, 0)
    scd_far = start(remote(scd.at[0], scd.at[2], sc_s.at[4], sc_r.at[4], far_dev))
    scd_sib = start(remote(scd.at[0], scd.at[1], sc_s.at[3], sc_r.at[3], sib_dev))
    dn_sib = start(remote(wdn.at[0], wdn.at[1], wd_s.at[0, 0], wd_r.at[0, 0], sib_dev))

    gu_fwd, dn_far, dn_fwd = [], [], []

    def forward_gu(p):
        gu_far[p].wait_recv()
        rows = part_rows(p)
        gu_fwd.append(
            start(remote(wgu.at[2, rows], wgu.at[3, rows], wg_s.at[2, p], wg_r.at[2, p], sib_dev))
        )

    def dn_rows(p):
        return pl.ds(p * 512, 512)

    def send_dn(p):
        rows = dn_rows(p)
        dn_far.append(
            start(remote(wdn.at[0, rows], wdn.at[2, rows], wd_s.at[1, p], wd_r.at[1, p], far_dev))
        )

    def forward_dn(p):
        dn_far[p].wait_recv()
        rows = dn_rows(p)
        dn_fwd.append(
            start(remote(wdn.at[2, rows], wdn.at[3, rows], wd_s.at[2, p], wd_r.at[2, p], sib_dev))
        )

    def gated(k, blocks, begin=False):
        def column_tile(n, carry):
            cols = pl.ds(pl.multiple_of(n * 256, 256), 256)
            total = None if begin else acc[:, cols]
            for b in blocks:
                inner = slice(b * 128, b * 128 + 128)
                piece = jnp.dot(
                    xr[k, :, inner], wgu[k, inner, cols], preferred_element_type=F32
                ) * scg[k, b : b + 1, cols]
                total = piece if total is None else total + piece
            acc[:, cols] = total
            return carry

        lax.fori_loop(0, GU // 256, column_tile, 0)

    arrived(0)
    gated(0, range(8), begin=True)
    forward_gu(0)
    scg_far.wait_recv()
    scg_fwd = start(remote(scg.at[2], scg.at[3], sc_s.at[2], sc_r.at[2], sib_dev))
    scg_sib.wait_recv()
    for p in range(PARTS):
        gu_sib[p].wait_recv()
    arrived(1)
    gated(1, range(8))
    forward_gu(1)
    arrived(2)
    gated(2, range(4))
    forward_gu(2)
    send_dn(0)
    gated(2, range(4, 6))
    arrived(3)
    scg_fwd.wait_recv()
    for p in range(3):
        gu_fwd[p].wait_recv()
    gated(3, range(6))
    forward_gu(3)
    send_dn(1)
    gated(2, range(6, 8))
    gu_fwd[3].wait_recv()
    gated(3, range(6, 8))

    def activate(n, carry):
        cols = pl.ds(pl.multiple_of(n * 256, 256), 256)
        gate = acc[:, cols]
        up = acc[:, pl.ds(pl.multiple_of(HW + n * 256, 256), 256)]
        hid[:, cols] = (gate / (1.0 + jnp.exp(-gate)) * up).astype(BF16)
        return carry

    lax.fori_loop(0, HW // 256, activate, 0)

    returned = []

    def lower(k):
        for copy in dispatched[k]:
            copy.wait_send()

        def row_tile(n, carry):
            cols = pl.ds(pl.multiple_of(n * 256, 256), 256)
            total = None
            for c in range(HW // 128):
                inner = slice(c * 128, c * 128 + 128)
                piece = lax.dot_general(
                    hid[:, inner],
                    wdn[k, cols, inner],
                    (((1,), (1,)), ((), ())),
                    preferred_element_type=F32,
                ) * scd[k, c : c + 1, cols]
                total = piece if total is None else total + piece
            og[k, :, cols] = total.astype(BF16)
            return carry

        lax.fori_loop(0, DC // 256, row_tile, 0)
        for i, (dev, p) in enumerate(peers):
            start(
                remote(
                    og.at[k, slot_rows(p)],
                    ret.at[k, slot_rows(pe)],
                    ret_s.at[k, i],
                    ret_r.at[k, i],
                    dev,
                )
            )
        copy = pltpu.make_async_copy(og.at[k, slot_rows(pe)], ret.at[k, slot_rows(pe)], ret_l.at[k])
        copy.start()
        returned.append(copy)

    partial = []

    def mix(k):
        returned[k].wait()
        for i, p in enumerate(sources):
            remote(
                og.at[k, slot_rows(p)],
                ret.at[k, slot_rows(p)],
                ret_s.at[k, i],
                ret_r.at[k, i],
                peers[i][0],
            ).wait_recv()

        def column_tile(n, carry):
            cols = pl.ds(pl.multiple_of(n * 256, 256), 256)
            other = jnp.dot(comb[TOK:, :], ret[k, :, cols], preferred_element_type=F32)
            ps[k, :, cols] = other.astype(BF16)
            return carry

        def own_tile(n, carry):
            cols = pl.ds(pl.multiple_of(n * 256, 256), 256)
            acc[k * TOK : (k + 1) * TOK, cols] = jnp.dot(
                comb[0:TOK, :], ret[k, :, cols], preferred_element_type=F32
            )
            return carry

        lax.fori_loop(0, DC // 256, column_tile, 0)
        partial.append(start(remote(ps.at[k], pr.at[k], par_s.at[k], par_r.at[k], from_dev)))
        lax.fori_loop(0, DC // 256, own_tile, 0)

    written = []

    def finish(k):
        partial[k].wait_recv()
        here = k + 2 * apart * (1 - 2 * (k // 2))
        rows = pl.ds(pl.multiple_of(here * TOK, TOK), TOK)
        tokv[k, 0:TOK, :] = (acc[rows, 0:DC] + pr[k].astype(F32)).astype(BF16)
        copy = pltpu.make_async_copy(
            tokv.at[k, pl.ds(0, TOK)], out.at[:, columns(zero_to, k)], out_sem.at[k]
        )
        copy.start()
        written.append(copy)

    for copy in tok_copy:
        copy.wait_send()
    lower(0)
    scd_sib.wait_recv()
    dn_sib.wait_recv()
    lower(1)
    scd_far.wait_recv()
    scd_fwd = start(remote(scd.at[2], scd.at[3], sc_s.at[5], sc_r.at[5], sib_dev))
    forward_dn(0)
    forward_dn(1)
    lower(2)
    scd_fwd.wait_recv()
    for p in range(2):
        dn_fwd[p].wait_recv()
    lower(3)
    mix(0)
    mix(1)
    mix(2)
    finish(0)
    mix(3)
    finish(2)
    finish(1)
    finish(3)
    for copy in sends:
        copy.wait_send()
    for copy in written:
        copy.wait()


def shards(*args):
    any_spec = pl.BlockSpec(memory_space=pl.ANY)
    vmem_spec = pl.BlockSpec(memory_space=pltpu.VMEM)
    dma = pltpu.SemaphoreType.DMA
    scratch = [
        pltpu.VMEM((CHUNKS, 2 * TOK, DC), BF16),
        pltpu.VMEM((2 * TOK, 128), F32),
        pltpu.VMEM((TOK, 128), F32),
        pltpu.VMEM((ROWS, 2 * TOK), BF16),
        pltpu.VMEM((2 * TOK, ROWS), BF16),
        pltpu.VMEM((CHUNKS, ROWS, DC), BF16),
        pltpu.VMEM((CHUNKS, ROWS, DC), BF16),
        pltpu.VMEM((4, SHARD, GU), BF16),
        pltpu.VMEM((4, SHARD, HW), BF16),
        pltpu.VMEM((4, 8, GU), F32),
        pltpu.VMEM((4, 8, SHARD), F32),
        pltpu.VMEM((ROWS, GU), F32),
        pltpu.VMEM((ROWS, HW), BF16),
        pltpu.VMEM((CHUNKS, ROWS, DC), BF16),
        pltpu.VMEM((CHUNKS, TOK, DC), BF16),
        pltpu.VMEM((CHUNKS, TOK, DC), BF16),
        pltpu.VMEM((2, 128, GU), F32),
        pltpu.VMEM((2, 128, GU), BF16),
        pltpu.VMEM((2, 128, GU), BF16),
        pltpu.VMEM((2, 128, GU), BF16),
        pltpu.VMEM((2, 128, HW), F32),
        pltpu.VMEM((2, 128, HW), BF16),
        pltpu.VMEM((2, 128, HW), BF16),
        pltpu.VMEM((2, 128, HW), BF16),
        pltpu.VMEM((8, GU), F32),
        dma((CHUNKS,)), dma((CHUNKS,)), dma((CHUNKS,)),
        dma, dma,
        dma((CHUNKS,)), dma((CHUNKS, PEERS)), dma((CHUNKS, PEERS)),
        dma((CHUNKS,)), dma((CHUNKS, PEERS)), dma((CHUNKS, PEERS)),
        dma((3, PARTS)), dma((3, PARTS)), dma((3, 2)), dma((3, 2)),
        dma((6,)), dma((6,)),
        dma((CHUNKS,)), dma((CHUNKS,)),
        dma((2, 4)), dma((2, 4)), dma((CHUNKS,)),
    ]
    return pl.pallas_call(
        kernel,
        name="layer",
        out_shape=jax.ShapeDtypeStruct((TOK, D), BF16),
        in_specs=[any_spec, vmem_spec, vmem_spec] + [any_spec] * 8,
        out_specs=any_spec,
        scratch_shapes=scratch,
        compiler_params=pltpu.CompilerParams(
            collective_id=0, has_side_effects=True, vmem_limit_bytes=60 * 1024 * 1024
        ),
        cost_estimate=pl.CostEstimate(
            flops=17_000_000_000, bytes_accessed=30_000_000, transcendentals=5_000_000
        ),
    )(args[0], args[1].T, args[2].T, *args[3:])


def solution(mesh):
    rows = P(("expert", "zero"), None)
    weight = P("expert", "zero", None)
    in_specs = (rows,) * 3 + (weight,) * 8
    return jax.shard_map(shards, mesh=mesh, in_specs=in_specs, out_specs=rows, check_vma=False)
```

```python
import jax
import jax.numpy as jnp
from jax import lax
from jax.experimental import pallas as pl
from jax.experimental.pallas import tpu as pltpu
from jax.sharding import PartitionSpec as P

MESH = pl.DeviceIdType.MESH
F32 = jnp.float32
BF16 = jnp.bfloat16

TOK = 192
D = 4096
CAP = 24
PAIR = 2 * CAP
PLANE = 16
ROWS = PLANE * PAIR
GU = 1536
HW = 768
SHARD = 1024
CHUNKS = 4
DC = D // CHUNKS
PART_AT = (0, 256, 512, 896, 1024)
PARTS = len(PART_AT) - 1

beta_one = 0.9
beta_two = 0.999
learn_rate = 0.002
adam_eps = 1e-08
corr_two = 0.63230457523

OFFSETS = (
    (2, 2), (1, 2), (3, 2), (2, 1), (2, 3), (1, 1), (3, 3), (1, 3), (3, 1),
    (2, 0), (0, 2), (1, 0), (3, 0), (0, 1), (0, 3),
)
PEERS = len(OFFSETS)


def remote(src, dst, send_sem, recv_sem, device):
    return pltpu.make_async_remote_copy(
        src_ref=src,
        dst_ref=dst,
        send_sem=send_sem,
        recv_sem=recv_sem,
        device_id=device,
        device_id_type=MESH,
    )


def chunk_of(zero, k):
    sibling = zero + 1 - 2 * (zero % 2)
    base = sibling if k % 2 else zero
    return (base + 2) % 4 if k >= 2 else base


def adam(master, grad, first, second):
    grads = grad.astype(F32)
    move = (learn_rate * beta_one) * first.astype(F32) + (learn_rate * (1.0 - beta_one)) * grads
    spread = (beta_two / corr_two) * second.astype(F32) + ((1.0 - beta_two) / corr_two) * grads * grads
    below = spread * lax.rsqrt(spread) + adam_eps
    inverse = pl.reciprocal(below, approx=True)
    inverse = inverse * (2.0 - below * inverse)
    return master - move * inverse


def fresh_chunk(master, grad, first, second, inv, slot, width, quant, put_scale):
    def update(r, best):
        rows = pl.ds(pl.multiple_of(r * 16, 16), 16)
        fresh = adam(master[slot, rows, :], grad[slot, rows, :], first[slot, rows, :], second[slot, rows, :])
        master[slot, rows, :] = fresh
        size = jnp.abs(fresh)
        return jnp.maximum(best, jnp.maximum(size[:8], size[8:]))

    best = lax.fori_loop(0, 8, update, jnp.zeros((8, width), F32))
    for b in range(width // 128):
        cols = slice(b * 128, b * 128 + 128)
        largest = jnp.max(jnp.max(best[:, cols], axis=0, keepdims=True), axis=1, keepdims=True)
        scale = ((largest + 1e-06) / 448.0).astype(BF16).astype(F32)
        put_scale(b, scale)
        inv[:, cols] = jnp.broadcast_to(1.0 / scale, (8, 128))

    def cast(r, carry):
        rows = pl.ds(pl.multiple_of(r * 16, 16), 16)
        quant(rows, (master[slot, rows, :] * inv[0:1, 0:width]).astype(BF16), r)
        return carry

    lax.fori_loop(0, 8, cast, 0)


def kernel(
    tokens, ids, weights,
    mgu, ggu, fgu, vgu, mdn, gdn, fdn, vdn,
    out,
    tokv, pk, pks, sel, comb, og, xr, wgu, wdn, scg, scd, acc, hid, ret, ps, pr,
    am, ag, af, av, bm, bg, bf, bv, inv,
    tok_l, tok_s, tok_r, pk_s, pk_r, dis_l, dis_s, dis_r, ret_l, ret_s, ret_r,
    wg_s, wg_r, wd_s, wd_r, sc_s, sc_r, par_s, par_r, a_sem, b_sem, out_sem,
):
    expert = lax.axis_index("expert")
    zero = lax.axis_index("zero")
    x, zz, yl = expert // 8, (expert // 2) % 4, expert % 2
    yh, core = zero // 2, zero % 2
    y = yh * 2 + yl
    pe = x * 4 + zz
    step = 1 - 2 * core

    def at(px, py, pz, pc):
        return (px * 8 + pz * 2 + py % 2, (py // 2) * 2 + pc)

    y_to, y_from = (y + step + 4) % 4, (y - step + 4) % 4
    to_dev = at(x, y_to, zz, core)
    from_dev = at(x, y_from, zz, core)
    sib_dev = at(x, y, zz, 1 - core)
    far_dev = at(x, (y + 2) % 4, zz, core)
    zero_to = (y_to // 2) * 2 + core

    peers = []
    sources = []
    for ax, az in OFFSETS:
        dx, dz = ax + (az - ax) * core, az + (ax - az) * core
        px, pz = (x + dx) % 4, (zz + dz) % 4
        qx, qz = (x + 4 - dx) % 4, (zz + 4 - dz) % 4
        peers.append((at(px, y, pz, core), px * 4 + pz))
        sources.append(qx * 4 + qz)

    def slot_rows(p):
        return pl.ds(pl.multiple_of(p * PAIR, 16), PAIR)

    def columns(zero_index, k):
        return pl.ds(pl.multiple_of(chunk_of(zero_index, k) * DC, DC), DC)

    barrier = pltpu.get_barrier_semaphore()
    greeted = [dev for dev, _ in peers] + [sib_dev, far_dev, to_dev, from_dev]
    for dev in greeted:
        pl.semaphore_signal(barrier, inc=1, device_id=dev, device_id_type=MESH)

    own_tok = []
    for k in range(CHUNKS):
        copy = pltpu.make_async_copy(
            tokens.at[:, columns(zero, k)], tokv.at[k, pl.ds(0, TOK)], tok_l.at[k]
        )
        copy.start()
        own_tok.append(copy)

    def gu_loads(chunk):
        slot = chunk % 2
        rows = pl.ds(pl.multiple_of(chunk * 128, 128), 128)
        return [
            pltpu.make_async_copy(src.at[0, rows], dst.at[slot], a_sem.at[slot, i])
            for i, (src, dst) in enumerate(((mgu, am), (ggu, ag), (fgu, af), (vgu, av)))
        ]

    def dn_loads(chunk):
        slot = chunk % 2
        rows = pl.ds(pl.multiple_of(chunk * 128, 128), 128)
        return [
            pltpu.make_async_copy(src.at[0, rows], dst.at[slot], b_sem.at[slot, i])
            for i, (src, dst) in enumerate(((mdn, bm), (gdn, bg), (fdn, bf), (vdn, bv)))
        ]

    for chunk in range(2):
        for copy in gu_loads(chunk):
            copy.start()
    for chunk in range(2):
        for copy in dn_loads(chunk):
            copy.start()

    lane = lax.broadcasted_iota(jnp.int32, (128, TOK), 0)
    mine = jnp.zeros((128, TOK), F32)
    theirs = jnp.zeros((128, TOK), F32)
    for k in range(8):
        named = ids[k : k + 1, :]
        weight = weights[k : k + 1, :].astype(F32)
        for other in range(2):
            row = yl if other == 0 else 1 - yl
            value = jnp.where(
                named == lane * 8 + 4 * row,
                weight,
                jnp.where(named == (lane - 64) * 8 + 4 * row, 1.0, 0.0),
            )
            if other == 0:
                mine = mine + value
            else:
                theirs = theirs + value
    pk[0:TOK, :] = jnp.transpose(mine)
    pks[...] = jnp.transpose(theirs)

    pl.semaphore_wait(barrier, len(greeted))

    sends = []

    def start(copy):
        copy.start()
        sends.append(copy)
        return copy

    apart = (y_to // 2 - yh) * (y_to // 2 - yh)
    for k in range(CHUNKS):
        own_tok[k].wait()
    pk_copy = start(remote(pks, pk.at[pl.ds(TOK, TOK)], pk_s, pk_r, to_dev))
    tok_copy = [
        remote(
                tokv.at[k + 2 * apart * (1 - 2 * (k // 2)), pl.ds(0, TOK)],
                tokv.at[k, pl.ds(TOK, TOK)],
                tok_s.at[k],
                tok_r.at[k],
                to_dev,
        )
        for k in range(CHUNKS)
    ]
    for copy in tok_copy:
        copy.start()

    eighth = lax.broadcasted_iota(jnp.int32, (8, 128), 0)
    scg[0] = jnp.zeros((8, GU), F32)
    scd[0] = jnp.zeros((8, SHARD), F32)

    def adam_gu(chunk, carry):
        for copy in gu_loads(chunk):
            copy.wait()

        def quant(rows, value, r):
            wgu[0, pl.ds(pl.multiple_of(chunk * 128 + r * 16, 16), 16), :] = value

        def put_scale(b, scale):
            cols = slice(b * 128, b * 128 + 128)
            scg[0, :, cols] = jnp.where(eighth == chunk, scale, scg[0, :, cols])

        fresh_chunk(am, ag, af, av, inv, chunk % 2, GU, quant, put_scale)

        @pl.when(chunk + 2 < SHARD // 128)
        def _():
            for copy in gu_loads(chunk + 2):
                copy.start()

        return carry

    def adam_dn(chunk, carry):
        for copy in dn_loads(chunk):
            copy.wait()
        cols = pl.ds(pl.multiple_of(chunk * 128, 128), 128)

        def quant(rows, value, r):
            wdn[0, pl.ds(pl.multiple_of(chunk * 128 + r * 16, 16), 16), :] = value

        def put_scale(b, scale):
            scd[0, b : b + 1, cols] = jnp.broadcast_to(scale, (1, 128))

        fresh_chunk(bm, bg, bf, bv, inv, chunk % 2, HW, quant, put_scale)

        @pl.when(chunk + 2 < SHARD // 128)
        def _():
            for copy in dn_loads(chunk + 2):
                copy.start()

        return carry

    def part_rows(p):
        return pl.ds(PART_AT[p], PART_AT[p + 1] - PART_AT[p])

    gu_sib, gu_far = [], []

    def send_gu(p):
        rows = part_rows(p)
        gu_far.append(
            start(remote(wgu.at[0, rows], wgu.at[2, rows], wg_s.at[1, p], wg_r.at[1, p], far_dev))
        )
        gu_sib.append(
            start(remote(wgu.at[0, rows], wgu.at[1, rows], wg_s.at[0, p], wg_r.at[0, p], sib_dev))
        )

    def build_maps():
        pk_copy.wait_recv()
        packed = pk[...]
        place = lax.broadcasted_iota(jnp.int32, (128, ROWS), 0)
        slot_no = lax.broadcasted_iota(jnp.int32, (128, ROWS), 1)
        lowest = (place - 64) * PAIR
        spread_slot = jnp.where((slot_no >= lowest) & (slot_no < lowest + PAIR), 1.0, 0.0).astype(BF16)
        low_weight = place * PAIR
        spread_weight = jnp.where(
            (slot_no >= low_weight) & (slot_no < low_weight + PAIR), 1.0, 0.0
        ).astype(BF16)
        t_row = lax.broadcasted_iota(jnp.int32, (2 * TOK, 2 * TOK), 0)
        t_col = lax.broadcasted_iota(jnp.int32, (2 * TOK, 2 * TOK), 1)
        same = (t_row >= TOK) == (t_col >= TOK)
        earlier = jnp.where((t_col < t_row) & same, 1.0, 0.0).astype(BF16)
        flags = packed.astype(BF16)
        counted = jnp.dot(earlier, flags, preferred_element_type=F32)
        token = lax.broadcasted_iota(jnp.int32, (2 * TOK, 128), 0)
        slot = counted + jnp.where(token >= TOK, float(CAP), 0.0)
        lanes = lax.broadcasted_iota(jnp.int32, (2 * TOK, 128), 1)
        chosen = (packed > 0.5) & (lanes >= 64)
        slot = jnp.where(chosen, slot, jnp.where(lanes >= 64, -1.0, 0.0)).astype(BF16)
        route = jnp.where(lanes < 64, packed, 0.0).astype(BF16)

        wide = lax.broadcasted_iota(jnp.int32, (1, ROWS), 1)
        within = wide
        for p in range(1, PLANE):
            within = within - jnp.where(wide >= p * PAIR, PAIR, 0)
        slots_wide = jnp.dot(slot, spread_slot, preferred_element_type=F32)
        route_wide = jnp.dot(route, spread_weight, preferred_element_type=F32)
        hit = slots_wide == within.astype(F32)
        comb[...] = jnp.where(hit, route_wide, 0.0).astype(BF16)
        sel[...] = jnp.transpose(jnp.where(hit, 1.0, 0.0)).astype(BF16)

    dispatched = [[] for _ in range(CHUNKS)]
    kept = []

    def dispatch(k, also=()):
        tok_copy[k].wait_recv()

        def column_tile(n, carry):
            cols = pl.ds(pl.multiple_of(n * 256, 256), 256)
            og[k, :, cols] = jnp.dot(
                sel[...], tokv[k, :, cols], preferred_element_type=F32
            ).astype(BF16)
            return carry

        lax.fori_loop(0, DC // 256, column_tile, 0)
        for i, (dev, p) in enumerate(peers):
            copy = remote(
                og.at[k, slot_rows(p)], xr.at[k, slot_rows(pe)], dis_s.at[k, i], dis_r.at[k, i], dev
            )
            copy.start()
            dispatched[k].append(copy)
            for p, after in also:
                if after == i:
                    send_gu(p)
        copy = pltpu.make_async_copy(og.at[k, slot_rows(pe)], xr.at[k, slot_rows(pe)], dis_l.at[k])
        copy.start()
        kept.append(copy)

    def arrived(k):
        kept[k].wait()
        for i, p in enumerate(sources):
            remote(
                og.at[k, slot_rows(p)],
                xr.at[k, slot_rows(p)],
                dis_s.at[k, i],
                dis_r.at[k, i],
                peers[i][0],
            ).wait_recv()

    lax.fori_loop(0, 2, adam_gu, 0)
    build_maps()
    dispatch(0)
    lax.fori_loop(2, 4, adam_gu, 0)
    dispatch(1)
    lax.fori_loop(4, 6, adam_gu, 0)
    dispatch(2)
    lax.fori_loop(6, 8, adam_gu, 0)
    send_gu(0)
    dispatch(3, ((1, 7),))
    scg_far = start(remote(scg.at[0], scg.at[2], sc_s.at[1], sc_r.at[1], far_dev))
    scg_sib = start(remote(scg.at[0], scg.at[1], sc_s.at[0], sc_r.at[0], sib_dev))
    send_gu(2)
    send_gu(3)
    lax.fori_loop(0, 8, adam_dn, 0)
    scd_far = start(remote(scd.at[0], scd.at[2], sc_s.at[4], sc_r.at[4], far_dev))
    scd_sib = start(remote(scd.at[0], scd.at[1], sc_s.at[3], sc_r.at[3], sib_dev))
    dn_sib = start(remote(wdn.at[0], wdn.at[1], wd_s.at[0, 0], wd_r.at[0, 0], sib_dev))

    gu_fwd, dn_far, dn_fwd = [], [], []

    def forward_gu(p):
        gu_far[p].wait_recv()
        rows = part_rows(p)
        gu_fwd.append(
            start(remote(wgu.at[2, rows], wgu.at[3, rows], wg_s.at[2, p], wg_r.at[2, p], sib_dev))
        )

    def dn_rows(p):
        return pl.ds(p * 512, 512)

    def send_dn(p):
        rows = dn_rows(p)
        dn_far.append(
            start(remote(wdn.at[0, rows], wdn.at[2, rows], wd_s.at[1, p], wd_r.at[1, p], far_dev))
        )

    def forward_dn(p):
        dn_far[p].wait_recv()
        rows = dn_rows(p)
        dn_fwd.append(
            start(remote(wdn.at[2, rows], wdn.at[3, rows], wd_s.at[2, p], wd_r.at[2, p], sib_dev))
        )

    def gated(k, blocks, begin=False):
        def column_tile(n, carry):
            cols = pl.ds(pl.multiple_of(n * 256, 256), 256)
            total = None if begin else acc[:, cols]
            for b in blocks:
                inner = slice(b * 128, b * 128 + 128)
                piece = jnp.dot(
                    xr[k, :, inner], wgu[k, inner, cols], preferred_element_type=F32
                ) * scg[k, b : b + 1, cols]
                total = piece if total is None else total + piece
            acc[:, cols] = total
            return carry

        lax.fori_loop(0, GU // 256, column_tile, 0)

    arrived(0)
    gated(0, range(8), begin=True)
    forward_gu(0)
    scg_far.wait_recv()
    scg_fwd = start(remote(scg.at[2], scg.at[3], sc_s.at[2], sc_r.at[2], sib_dev))
    scg_sib.wait_recv()
    for p in range(PARTS):
        gu_sib[p].wait_recv()
    arrived(1)
    gated(1, range(8))
    forward_gu(1)
    arrived(2)
    gated(2, range(4))
    forward_gu(2)
    send_dn(0)
    gated(2, range(4, 7))
    arrived(3)
    scg_fwd.wait_recv()
    for p in range(3):
        gu_fwd[p].wait_recv()
    gated(3, range(7))
    forward_gu(3)
    send_dn(1)
    gated(2, range(7, 8))
    gu_fwd[3].wait_recv()
    gated(3, range(7, 8))

    def activate(n, carry):
        cols = pl.ds(pl.multiple_of(n * 256, 256), 256)
        gate = acc[:, cols]
        up = acc[:, pl.ds(pl.multiple_of(HW + n * 256, 256), 256)]
        hid[:, cols] = (gate / (1.0 + jnp.exp(-gate)) * up).astype(BF16)
        return carry

    lax.fori_loop(0, HW // 256, activate, 0)

    returned = []

    def lower(k):
        for copy in dispatched[k]:
            copy.wait_send()

        def row_tile(n, carry):
            cols = pl.ds(pl.multiple_of(n * 256, 256), 256)
            total = None
            for c in range(HW // 128):
                inner = slice(c * 128, c * 128 + 128)
                piece = lax.dot_general(
                    hid[:, inner],
                    wdn[k, cols, inner],
                    (((1,), (1,)), ((), ())),
                    preferred_element_type=F32,
                ) * scd[k, c : c + 1, cols]
                total = piece if total is None else total + piece
            og[k, :, cols] = total.astype(BF16)
            return carry

        lax.fori_loop(0, DC // 256, row_tile, 0)
        for i, (dev, p) in enumerate(peers):
            start(
                remote(
                    og.at[k, slot_rows(p)],
                    ret.at[k, slot_rows(pe)],
                    ret_s.at[k, i],
                    ret_r.at[k, i],
                    dev,
                )
            )
        copy = pltpu.make_async_copy(og.at[k, slot_rows(pe)], ret.at[k, slot_rows(pe)], ret_l.at[k])
        copy.start()
        returned.append(copy)

    partial = []

    def mix(k):
        returned[k].wait()
        for i, p in enumerate(sources):
            remote(
                og.at[k, slot_rows(p)],
                ret.at[k, slot_rows(p)],
                ret_s.at[k, i],
                ret_r.at[k, i],
                peers[i][0],
            ).wait_recv()

        def column_tile(n, carry):
            cols = pl.ds(pl.multiple_of(n * 256, 256), 256)
            other = jnp.dot(comb[TOK:, :], ret[k, :, cols], preferred_element_type=F32)
            ps[k, :, cols] = other.astype(BF16)
            return carry

        def own_tile(n, carry):
            cols = pl.ds(pl.multiple_of(n * 256, 256), 256)
            acc[k * TOK : (k + 1) * TOK, cols] = jnp.dot(
                comb[0:TOK, :], ret[k, :, cols], preferred_element_type=F32
            )
            return carry

        halves = []
        for h in range(2):
            lax.fori_loop(2 * h, 2 * h + 2, column_tile, 0)
            cols = pl.ds(h * 512, 512)
            halves.append(
                start(
                    remote(
                        ps.at[k, :, cols], pr.at[k, :, cols], par_s.at[k, h], par_r.at[k, h], from_dev
                    )
                )
            )
        partial.append(halves)
        lax.fori_loop(0, DC // 256, own_tile, 0)

    written = []

    def finish(k):
        here = k + 2 * apart * (1 - 2 * (k // 2))
        rows = pl.ds(pl.multiple_of(here * TOK, TOK), TOK)
        for h in range(2):
            partial[k][h].wait_recv()
            cols = slice(h * 512, h * 512 + 512)
            tokv[k, 0:TOK, cols] = (acc[rows, cols] + pr[k, :, cols].astype(F32)).astype(BF16)
        copy = pltpu.make_async_copy(
            tokv.at[k, pl.ds(0, TOK)], out.at[:, columns(zero_to, k)], out_sem.at[k]
        )
        copy.start()
        written.append(copy)

    for copy in tok_copy:
        copy.wait_send()
    lower(0)
    scd_sib.wait_recv()
    dn_sib.wait_recv()
    lower(1)
    scd_far.wait_recv()
    scd_fwd = start(remote(scd.at[2], scd.at[3], sc_s.at[5], sc_r.at[5], sib_dev))
    forward_dn(0)
    forward_dn(1)
    lower(2)
    scd_fwd.wait_recv()
    for p in range(2):
        dn_fwd[p].wait_recv()
    lower(3)
    mix(0)
    mix(1)
    mix(2)
    finish(0)
    mix(3)
    finish(2)
    finish(1)
    finish(3)
    for copy in sends:
        copy.wait_send()
    for copy in written:
        copy.wait()


def shards(*args):
    any_spec = pl.BlockSpec(memory_space=pl.ANY)
    vmem_spec = pl.BlockSpec(memory_space=pltpu.VMEM)
    dma = pltpu.SemaphoreType.DMA
    scratch = [
        pltpu.VMEM((CHUNKS, 2 * TOK, DC), BF16),
        pltpu.VMEM((2 * TOK, 128), F32),
        pltpu.VMEM((TOK, 128), F32),
        pltpu.VMEM((ROWS, 2 * TOK), BF16),
        pltpu.VMEM((2 * TOK, ROWS), BF16),
        pltpu.VMEM((CHUNKS, ROWS, DC), BF16),
        pltpu.VMEM((CHUNKS, ROWS, DC), BF16),
        pltpu.VMEM((4, SHARD, GU), BF16),
        pltpu.VMEM((4, SHARD, HW), BF16),
        pltpu.VMEM((4, 8, GU), F32),
        pltpu.VMEM((4, 8, SHARD), F32),
        pltpu.VMEM((ROWS, GU), F32),
        pltpu.VMEM((ROWS, HW), BF16),
        pltpu.VMEM((CHUNKS, ROWS, DC), BF16),
        pltpu.VMEM((CHUNKS, TOK, DC), BF16),
        pltpu.VMEM((CHUNKS, TOK, DC), BF16),
        pltpu.VMEM((2, 128, GU), F32),
        pltpu.VMEM((2, 128, GU), BF16),
        pltpu.VMEM((2, 128, GU), BF16),
        pltpu.VMEM((2, 128, GU), BF16),
        pltpu.VMEM((2, 128, HW), F32),
        pltpu.VMEM((2, 128, HW), BF16),
        pltpu.VMEM((2, 128, HW), BF16),
        pltpu.VMEM((2, 128, HW), BF16),
        pltpu.VMEM((8, GU), F32),
        dma((CHUNKS,)), dma((CHUNKS,)), dma((CHUNKS,)),
        dma, dma,
        dma((CHUNKS,)), dma((CHUNKS, PEERS)), dma((CHUNKS, PEERS)),
        dma((CHUNKS,)), dma((CHUNKS, PEERS)), dma((CHUNKS, PEERS)),
        dma((3, PARTS)), dma((3, PARTS)), dma((3, 2)), dma((3, 2)),
        dma((6,)), dma((6,)),
        dma((CHUNKS, 2)), dma((CHUNKS, 2)),
        dma((2, 4)), dma((2, 4)), dma((CHUNKS,)),
    ]
    return pl.pallas_call(
        kernel,
        name="layer",
        out_shape=jax.ShapeDtypeStruct((TOK, D), BF16),
        in_specs=[any_spec, vmem_spec, vmem_spec] + [any_spec] * 8,
        out_specs=any_spec,
        scratch_shapes=scratch,
        compiler_params=pltpu.CompilerParams(
            collective_id=0, has_side_effects=True, vmem_limit_bytes=60 * 1024 * 1024
        ),
        cost_estimate=pl.CostEstimate(
            flops=17_000_000_000, bytes_accessed=30_000_000, transcendentals=5_000_000
        ),
    )(args[0], args[1].T, args[2].T, *args[3:])


def solution(mesh):
    rows = P(("expert", "zero"), None)
    weight = P("expert", "zero", None)
    in_specs = (rows,) * 3 + (weight,) * 8
    return jax.shard_map(shards, mesh=mesh, in_specs=in_specs, out_specs=rows, check_vma=False)
```

```python
import jax
import jax.numpy as jnp
from jax import lax
from jax.experimental import pallas as pl
from jax.experimental.pallas import tpu as pltpu
from jax.sharding import PartitionSpec as P

MESH = pl.DeviceIdType.MESH
F32 = jnp.float32
BF16 = jnp.bfloat16

TOK = 192
D = 4096
CAP = 24
PAIR = 2 * CAP
PLANE = 16
ROWS = PLANE * PAIR
GU = 1536
HW = 768
SHARD = 1024
CHUNKS = 4
DC = D // CHUNKS
PART_AT = (0, 256, 512, 896, 1024)
PARTS = len(PART_AT) - 1

beta_one = 0.9
beta_two = 0.999
learn_rate = 0.002
adam_eps = 1e-08
corr_two = 0.63230457523

OFFSETS = (
    (2, 2), (1, 2), (3, 2), (2, 1), (2, 3), (1, 1), (3, 3), (1, 3), (3, 1),
    (2, 0), (0, 2), (1, 0), (3, 0), (0, 1), (0, 3),
)
PEERS = len(OFFSETS)


def remote(src, dst, send_sem, recv_sem, device):
    return pltpu.make_async_remote_copy(
        src_ref=src,
        dst_ref=dst,
        send_sem=send_sem,
        recv_sem=recv_sem,
        device_id=device,
        device_id_type=MESH,
    )


def chunk_of(zero, k):
    sibling = zero + 1 - 2 * (zero % 2)
    base = sibling if k % 2 else zero
    return (base + 2) % 4 if k >= 2 else base


def adam(master, grad, first, second):
    grads = grad.astype(F32)
    move = (learn_rate * beta_one) * first.astype(F32) + (learn_rate * (1.0 - beta_one)) * grads
    spread = (beta_two / corr_two) * second.astype(F32) + ((1.0 - beta_two) / corr_two) * grads * grads
    below = spread * lax.rsqrt(spread) + adam_eps
    inverse = pl.reciprocal(below, approx=True)
    inverse = inverse * (2.0 - below * inverse)
    return master - move * inverse


def fresh_chunk(master, grad, first, second, inv, slot, width, quant, put_scale):
    def update(r, best):
        rows = pl.ds(pl.multiple_of(r * 16, 16), 16)
        fresh = adam(master[slot, rows, :], grad[slot, rows, :], first[slot, rows, :], second[slot, rows, :])
        master[slot, rows, :] = fresh
        size = jnp.abs(fresh)
        return jnp.maximum(best, jnp.maximum(size[:8], size[8:]))

    best = lax.fori_loop(0, 8, update, jnp.zeros((8, width), F32))
    for b in range(width // 128):
        cols = slice(b * 128, b * 128 + 128)
        largest = jnp.max(jnp.max(best[:, cols], axis=0, keepdims=True), axis=1, keepdims=True)
        scale = ((largest + 1e-06) / 448.0).astype(BF16).astype(F32)
        put_scale(b, scale)
        inv[:, cols] = jnp.broadcast_to(1.0 / scale, (8, 128))

    def cast(r, carry):
        rows = pl.ds(pl.multiple_of(r * 16, 16), 16)
        quant(rows, (master[slot, rows, :] * inv[0:1, 0:width]).astype(BF16), r)
        return carry

    lax.fori_loop(0, 8, cast, 0)


def kernel(
    tokens, ids, weights,
    mgu, ggu, fgu, vgu, mdn, gdn, fdn, vdn,
    out,
    tokv, pk, pks, sel, comb, og, xr, wgu, wdn, scg, scd, acc, hid, ret, ps, pr,
    am, ag, af, av, bm, bg, bf, bv, inv,
    tok_l, tok_s, tok_r, pk_s, pk_r, dis_l, dis_s, dis_r, ret_l, ret_s, ret_r,
    wg_s, wg_r, wd_s, wd_r, sc_s, sc_r, par_s, par_r, a_sem, b_sem, out_sem,
):
    expert = lax.axis_index("expert")
    zero = lax.axis_index("zero")
    x, zz, yl = expert // 8, (expert // 2) % 4, expert % 2
    yh, core = zero // 2, zero % 2
    y = yh * 2 + yl
    pe = x * 4 + zz
    step = 1 - 2 * core

    def at(px, py, pz, pc):
        return (px * 8 + pz * 2 + py % 2, (py // 2) * 2 + pc)

    y_to, y_from = (y + step + 4) % 4, (y - step + 4) % 4
    to_dev = at(x, y_to, zz, core)
    from_dev = at(x, y_from, zz, core)
    sib_dev = at(x, y, zz, 1 - core)
    far_dev = at(x, (y + 2) % 4, zz, core)
    zero_to = (y_to // 2) * 2 + core

    peers = []
    sources = []
    for ax, az in OFFSETS:
        dx, dz = ax + (az - ax) * core, az + (ax - az) * core
        px, pz = (x + dx) % 4, (zz + dz) % 4
        qx, qz = (x + 4 - dx) % 4, (zz + 4 - dz) % 4
        peers.append((at(px, y, pz, core), px * 4 + pz))
        sources.append(qx * 4 + qz)

    def slot_rows(p):
        return pl.ds(pl.multiple_of(p * PAIR, 16), PAIR)

    def columns(zero_index, k):
        return pl.ds(pl.multiple_of(chunk_of(zero_index, k) * DC, DC), DC)

    barrier = pltpu.get_barrier_semaphore()
    greeted = [dev for dev, _ in peers] + [sib_dev, far_dev, to_dev, from_dev]
    for dev in greeted:
        pl.semaphore_signal(barrier, inc=1, device_id=dev, device_id_type=MESH)

    own_tok = []
    for k in range(CHUNKS):
        copy = pltpu.make_async_copy(
            tokens.at[:, columns(zero, k)], tokv.at[k, pl.ds(0, TOK)], tok_l.at[k]
        )
        copy.start()
        own_tok.append(copy)

    def gu_loads(chunk):
        slot = chunk % 2
        rows = pl.ds(pl.multiple_of(chunk * 128, 128), 128)
        return [
            pltpu.make_async_copy(src.at[0, rows], dst.at[slot], a_sem.at[slot, i])
            for i, (src, dst) in enumerate(((mgu, am), (ggu, ag), (fgu, af), (vgu, av)))
        ]

    def dn_loads(chunk):
        slot = chunk % 2
        rows = pl.ds(pl.multiple_of(chunk * 128, 128), 128)
        return [
            pltpu.make_async_copy(src.at[0, rows], dst.at[slot], b_sem.at[slot, i])
            for i, (src, dst) in enumerate(((mdn, bm), (gdn, bg), (fdn, bf), (vdn, bv)))
        ]

    for chunk in range(2):
        for copy in gu_loads(chunk):
            copy.start()
    for chunk in range(2):
        for copy in dn_loads(chunk):
            copy.start()

    lane = lax.broadcasted_iota(jnp.int32, (128, TOK), 0)
    mine = jnp.zeros((128, TOK), F32)
    theirs = jnp.zeros((128, TOK), F32)
    for k in range(8):
        named = ids[k : k + 1, :]
        weight = weights[k : k + 1, :].astype(F32)
        for other in range(2):
            row = yl if other == 0 else 1 - yl
            value = jnp.where(
                named == lane * 8 + 4 * row,
                weight,
                jnp.where(named == (lane - 64) * 8 + 4 * row, 1.0, 0.0),
            )
            if other == 0:
                mine = mine + value
            else:
                theirs = theirs + value
    pk[0:TOK, :] = jnp.transpose(mine)
    pks[...] = jnp.transpose(theirs)

    pl.semaphore_wait(barrier, len(greeted))

    sends = []

    def start(copy):
        copy.start()
        sends.append(copy)
        return copy

    apart = (y_to // 2 - yh) * (y_to // 2 - yh)
    for k in range(CHUNKS):
        own_tok[k].wait()
    pk_copy = start(remote(pks, pk.at[pl.ds(TOK, TOK)], pk_s, pk_r, to_dev))
    tok_copy = [
        remote(
                tokv.at[k + 2 * apart * (1 - 2 * (k // 2)), pl.ds(0, TOK)],
                tokv.at[k, pl.ds(TOK, TOK)],
                tok_s.at[k],
                tok_r.at[k],
                to_dev,
        )
        for k in range(CHUNKS)
    ]
    for copy in tok_copy:
        copy.start()

    eighth = lax.broadcasted_iota(jnp.int32, (8, 128), 0)
    scg[0] = jnp.zeros((8, GU), F32)
    scd[0] = jnp.zeros((8, SHARD), F32)

    def adam_gu(chunk, carry):
        for copy in gu_loads(chunk):
            copy.wait()

        def quant(rows, value, r):
            wgu[0, pl.ds(pl.multiple_of(chunk * 128 + r * 16, 16), 16), :] = value

        def put_scale(b, scale):
            cols = slice(b * 128, b * 128 + 128)
            scg[0, :, cols] = jnp.where(eighth == chunk, scale, scg[0, :, cols])

        fresh_chunk(am, ag, af, av, inv, chunk % 2, GU, quant, put_scale)

        @pl.when(chunk + 2 < SHARD // 128)
        def _():
            for copy in gu_loads(chunk + 2):
                copy.start()

        return carry

    def adam_dn(chunk, carry):
        for copy in dn_loads(chunk):
            copy.wait()
        cols = pl.ds(pl.multiple_of(chunk * 128, 128), 128)

        def quant(rows, value, r):
            wdn[0, pl.ds(pl.multiple_of(chunk * 128 + r * 16, 16), 16), :] = value

        def put_scale(b, scale):
            scd[0, b : b + 1, cols] = jnp.broadcast_to(scale, (1, 128))

        fresh_chunk(bm, bg, bf, bv, inv, chunk % 2, HW, quant, put_scale)

        @pl.when(chunk + 2 < SHARD // 128)
        def _():
            for copy in dn_loads(chunk + 2):
                copy.start()

        return carry

    def part_rows(p):
        return pl.ds(PART_AT[p], PART_AT[p + 1] - PART_AT[p])

    gu_sib, gu_far = [], []

    def send_gu(p):
        rows = part_rows(p)
        gu_far.append(
            start(remote(wgu.at[0, rows], wgu.at[2, rows], wg_s.at[1, p], wg_r.at[1, p], far_dev))
        )
        gu_sib.append(
            start(remote(wgu.at[0, rows], wgu.at[1, rows], wg_s.at[0, p], wg_r.at[0, p], sib_dev))
        )

    def build_maps():
        pk_copy.wait_recv()
        packed = pk[...]
        place = lax.broadcasted_iota(jnp.int32, (128, ROWS), 0)
        slot_no = lax.broadcasted_iota(jnp.int32, (128, ROWS), 1)
        lowest = (place - 64) * PAIR
        spread_slot = jnp.where((slot_no >= lowest) & (slot_no < lowest + PAIR), 1.0, 0.0).astype(BF16)
        low_weight = place * PAIR
        spread_weight = jnp.where(
            (slot_no >= low_weight) & (slot_no < low_weight + PAIR), 1.0, 0.0
        ).astype(BF16)
        t_row = lax.broadcasted_iota(jnp.int32, (2 * TOK, 2 * TOK), 0)
        t_col = lax.broadcasted_iota(jnp.int32, (2 * TOK, 2 * TOK), 1)
        same = (t_row >= TOK) == (t_col >= TOK)
        earlier = jnp.where((t_col < t_row) & same, 1.0, 0.0).astype(BF16)
        flags = packed.astype(BF16)
        counted = jnp.dot(earlier, flags, preferred_element_type=F32)
        token = lax.broadcasted_iota(jnp.int32, (2 * TOK, 128), 0)
        slot = counted + jnp.where(token >= TOK, float(CAP), 0.0)
        lanes = lax.broadcasted_iota(jnp.int32, (2 * TOK, 128), 1)
        chosen = (packed > 0.5) & (lanes >= 64)
        slot = jnp.where(chosen, slot, jnp.where(lanes >= 64, -1.0, 0.0)).astype(BF16)
        route = jnp.where(lanes < 64, packed, 0.0).astype(BF16)

        wide = lax.broadcasted_iota(jnp.int32, (1, ROWS), 1)
        within = wide
        for p in range(1, PLANE):
            within = within - jnp.where(wide >= p * PAIR, PAIR, 0)
        slots_wide = jnp.dot(slot, spread_slot, preferred_element_type=F32)
        route_wide = jnp.dot(route, spread_weight, preferred_element_type=F32)
        hit = slots_wide == within.astype(F32)
        comb[...] = jnp.where(hit, route_wide, 0.0).astype(BF16)
        sel[...] = jnp.transpose(jnp.where(hit, 1.0, 0.0)).astype(BF16)

    dispatched = [[] for _ in range(CHUNKS)]
    kept = []

    def dispatch(k, also=()):
        tok_copy[k].wait_recv()

        def column_tile(n, carry):
            cols = pl.ds(pl.multiple_of(n * 256, 256), 256)
            og[k, :, cols] = jnp.dot(
                sel[...], tokv[k, :, cols], preferred_element_type=F32
            ).astype(BF16)
            return carry

        lax.fori_loop(0, DC // 256, column_tile, 0)
        for i, (dev, p) in enumerate(peers):
            copy = remote(
                og.at[k, slot_rows(p)], xr.at[k, slot_rows(pe)], dis_s.at[k, i], dis_r.at[k, i], dev
            )
            copy.start()
            dispatched[k].append(copy)
            for p, after in also:
                if after == i:
                    send_gu(p)
        copy = pltpu.make_async_copy(og.at[k, slot_rows(pe)], xr.at[k, slot_rows(pe)], dis_l.at[k])
        copy.start()
        kept.append(copy)

    def arrived(k):
        kept[k].wait()
        for i, p in enumerate(sources):
            remote(
                og.at[k, slot_rows(p)],
                xr.at[k, slot_rows(p)],
                dis_s.at[k, i],
                dis_r.at[k, i],
                peers[i][0],
            ).wait_recv()

    lax.fori_loop(0, 2, adam_gu, 0)
    build_maps()
    dispatch(0)
    lax.fori_loop(2, 4, adam_gu, 0)
    dispatch(1)
    lax.fori_loop(4, 6, adam_gu, 0)
    dispatch(2)
    lax.fori_loop(6, 8, adam_gu, 0)
    send_gu(0)
    dispatch(3, ((1, 7),))
    scg_far = start(remote(scg.at[0], scg.at[2], sc_s.at[1], sc_r.at[1], far_dev))
    scg_sib = start(remote(scg.at[0], scg.at[1], sc_s.at[0], sc_r.at[0], sib_dev))
    send_gu(2)
    send_gu(3)
    lax.fori_loop(0, 8, adam_dn, 0)
    scd_far = start(remote(scd.at[0], scd.at[2], sc_s.at[4], sc_r.at[4], far_dev))
    scd_sib = start(remote(scd.at[0], scd.at[1], sc_s.at[3], sc_r.at[3], sib_dev))
    dn_sib = start(remote(wdn.at[0], wdn.at[1], wd_s.at[0, 0], wd_r.at[0, 0], sib_dev))

    gu_fwd, dn_far, dn_fwd = [], [], []

    def forward_gu(p):
        gu_far[p].wait_recv()
        rows = part_rows(p)
        gu_fwd.append(
            start(remote(wgu.at[2, rows], wgu.at[3, rows], wg_s.at[2, p], wg_r.at[2, p], sib_dev))
        )

    def dn_rows(p):
        return pl.ds(p * 512, 512)

    def send_dn(p):
        rows = dn_rows(p)
        dn_far.append(
            start(remote(wdn.at[0, rows], wdn.at[2, rows], wd_s.at[1, p], wd_r.at[1, p], far_dev))
        )

    def forward_dn(p):
        dn_far[p].wait_recv()
        rows = dn_rows(p)
        dn_fwd.append(
            start(remote(wdn.at[2, rows], wdn.at[3, rows], wd_s.at[2, p], wd_r.at[2, p], sib_dev))
        )

    def gated(k, blocks, begin=False):
        def column_tile(n, carry):
            cols = pl.ds(pl.multiple_of(n * 256, 256), 256)
            total = None if begin else acc[:, cols]
            for b in blocks:
                inner = slice(b * 128, b * 128 + 128)
                piece = jnp.dot(
                    xr[k, :, inner], wgu[k, inner, cols], preferred_element_type=F32
                ) * scg[k, b : b + 1, cols]
                total = piece if total is None else total + piece
            acc[:, cols] = total
            return carry

        lax.fori_loop(0, GU // 256, column_tile, 0)

    arrived(0)
    gated(0, range(8), begin=True)
    forward_gu(0)
    scg_far.wait_recv()
    scg_fwd = start(remote(scg.at[2], scg.at[3], sc_s.at[2], sc_r.at[2], sib_dev))
    scg_sib.wait_recv()
    for p in range(PARTS):
        gu_sib[p].wait_recv()
    arrived(1)
    gated(1, range(8))
    forward_gu(1)
    arrived(2)
    gated(2, range(4))
    forward_gu(2)
    send_dn(0)
    gated(2, range(4, 7))
    arrived(3)
    scg_fwd.wait_recv()
    for p in range(3):
        gu_fwd[p].wait_recv()
    gated(3, range(7))
    forward_gu(3)
    send_dn(1)
    gated(2, range(7, 8))
    gu_fwd[3].wait_recv()
    gated(3, range(7, 8))

    def activate(n, carry):
        cols = pl.ds(pl.multiple_of(n * 256, 256), 256)
        gate = acc[:, cols]
        up = acc[:, pl.ds(pl.multiple_of(HW + n * 256, 256), 256)]
        hid[:, cols] = (gate / (1.0 + jnp.exp(-gate)) * up).astype(BF16)
        return carry

    lax.fori_loop(0, HW // 256, activate, 0)

    returned = []

    def lower(k):
        for copy in dispatched[k]:
            copy.wait_send()

        def row_tile(n, carry):
            cols = pl.ds(pl.multiple_of(n * 256, 256), 256)
            total = None
            for c in range(HW // 128):
                inner = slice(c * 128, c * 128 + 128)
                piece = lax.dot_general(
                    hid[:, inner],
                    wdn[k, cols, inner],
                    (((1,), (1,)), ((), ())),
                    preferred_element_type=F32,
                ) * scd[k, c : c + 1, cols]
                total = piece if total is None else total + piece
            og[k, :, cols] = total.astype(BF16)
            return carry

        pieces = 2 if k == CHUNKS - 1 else 1
        local = []
        for h in range(pieces):
            tiles = DC // 256 // pieces
            lax.fori_loop(h * tiles, (h + 1) * tiles, row_tile, 0)
            cols = pl.ds(h * (DC // pieces), DC // pieces)
            for i, (dev, p) in enumerate(peers):
                start(
                    remote(
                        og.at[k, slot_rows(p), cols],
                        ret.at[k, slot_rows(pe), cols],
                        ret_s.at[k + h, i],
                        ret_r.at[k + h, i],
                        dev,
                    )
                )
            copy = pltpu.make_async_copy(
                og.at[k, slot_rows(pe), cols], ret.at[k, slot_rows(pe), cols], ret_l.at[k + h]
            )
            copy.start()
            local.append(copy)
        returned.append(local)

    partial = []

    def mix(k):
        pieces = len(returned[k])

        def returns_in(h):
            returned[k][h].wait()
            cols = pl.ds(h * (DC // pieces), DC // pieces)
            for i, p in enumerate(sources):
                remote(
                    og.at[k, slot_rows(p), cols],
                    ret.at[k, slot_rows(p), cols],
                    ret_s.at[k + h, i],
                    ret_r.at[k + h, i],
                    peers[i][0],
                ).wait_recv()

        def column_tile(n, carry):
            cols = pl.ds(pl.multiple_of(n * 256, 256), 256)
            other = jnp.dot(comb[TOK:, :], ret[k, :, cols], preferred_element_type=F32)
            ps[k, :, cols] = other.astype(BF16)
            return carry

        def own_tile(n, carry):
            cols = pl.ds(pl.multiple_of(n * 256, 256), 256)
            acc[k * TOK : (k + 1) * TOK, cols] = jnp.dot(
                comb[0:TOK, :], ret[k, :, cols], preferred_element_type=F32
            )
            return carry

        halves = []
        for h in range(2):
            if h < pieces:
                returns_in(h)
            lax.fori_loop(2 * h, 2 * h + 2, column_tile, 0)
            cols = pl.ds(h * 512, 512)
            halves.append(
                start(
                    remote(
                        ps.at[k, :, cols], pr.at[k, :, cols], par_s.at[k, h], par_r.at[k, h], from_dev
                    )
                )
            )
        partial.append(halves)
        lax.fori_loop(0, DC // 256, own_tile, 0)

    written = []

    def finish(k):
        here = k + 2 * apart * (1 - 2 * (k // 2))
        rows = pl.ds(pl.multiple_of(here * TOK, TOK), TOK)
        for h in range(2):
            partial[k][h].wait_recv()
            cols = slice(h * 512, h * 512 + 512)
            tokv[k, 0:TOK, cols] = (acc[rows, cols] + pr[k, :, cols].astype(F32)).astype(BF16)
        copy = pltpu.make_async_copy(
            tokv.at[k, pl.ds(0, TOK)], out.at[:, columns(zero_to, k)], out_sem.at[k]
        )
        copy.start()
        written.append(copy)

    for copy in tok_copy:
        copy.wait_send()
    lower(0)
    scd_sib.wait_recv()
    dn_sib.wait_recv()
    lower(1)
    scd_far.wait_recv()
    scd_fwd = start(remote(scd.at[2], scd.at[3], sc_s.at[5], sc_r.at[5], sib_dev))
    forward_dn(0)
    forward_dn(1)
    lower(2)
    scd_fwd.wait_recv()
    for p in range(2):
        dn_fwd[p].wait_recv()
    lower(3)
    mix(0)
    mix(1)
    mix(2)
    finish(0)
    mix(3)
    finish(2)
    finish(1)
    finish(3)
    for copy in sends:
        copy.wait_send()
    for copy in written:
        copy.wait()


def shards(*args):
    any_spec = pl.BlockSpec(memory_space=pl.ANY)
    vmem_spec = pl.BlockSpec(memory_space=pltpu.VMEM)
    dma = pltpu.SemaphoreType.DMA
    scratch = [
        pltpu.VMEM((CHUNKS, 2 * TOK, DC), BF16),
        pltpu.VMEM((2 * TOK, 128), F32),
        pltpu.VMEM((TOK, 128), F32),
        pltpu.VMEM((ROWS, 2 * TOK), BF16),
        pltpu.VMEM((2 * TOK, ROWS), BF16),
        pltpu.VMEM((CHUNKS, ROWS, DC), BF16),
        pltpu.VMEM((CHUNKS, ROWS, DC), BF16),
        pltpu.VMEM((4, SHARD, GU), BF16),
        pltpu.VMEM((4, SHARD, HW), BF16),
        pltpu.VMEM((4, 8, GU), F32),
        pltpu.VMEM((4, 8, SHARD), F32),
        pltpu.VMEM((ROWS, GU), F32),
        pltpu.VMEM((ROWS, HW), BF16),
        pltpu.VMEM((CHUNKS, ROWS, DC), BF16),
        pltpu.VMEM((CHUNKS, TOK, DC), BF16),
        pltpu.VMEM((CHUNKS, TOK, DC), BF16),
        pltpu.VMEM((2, 128, GU), F32),
        pltpu.VMEM((2, 128, GU), BF16),
        pltpu.VMEM((2, 128, GU), BF16),
        pltpu.VMEM((2, 128, GU), BF16),
        pltpu.VMEM((2, 128, HW), F32),
        pltpu.VMEM((2, 128, HW), BF16),
        pltpu.VMEM((2, 128, HW), BF16),
        pltpu.VMEM((2, 128, HW), BF16),
        pltpu.VMEM((8, GU), F32),
        dma((CHUNKS,)), dma((CHUNKS,)), dma((CHUNKS,)),
        dma, dma,
        dma((CHUNKS,)), dma((CHUNKS, PEERS)), dma((CHUNKS, PEERS)),
        dma((CHUNKS + 1,)), dma((CHUNKS + 1, PEERS)), dma((CHUNKS + 1, PEERS)),
        dma((3, PARTS)), dma((3, PARTS)), dma((3, 2)), dma((3, 2)),
        dma((6,)), dma((6,)),
        dma((CHUNKS, 2)), dma((CHUNKS, 2)),
        dma((2, 4)), dma((2, 4)), dma((CHUNKS,)),
    ]
    return pl.pallas_call(
        kernel,
        name="layer",
        out_shape=jax.ShapeDtypeStruct((TOK, D), BF16),
        in_specs=[any_spec, vmem_spec, vmem_spec] + [any_spec] * 8,
        out_specs=any_spec,
        scratch_shapes=scratch,
        compiler_params=pltpu.CompilerParams(
            collective_id=0, has_side_effects=True, vmem_limit_bytes=60 * 1024 * 1024
        ),
        cost_estimate=pl.CostEstimate(
            flops=17_000_000_000, bytes_accessed=30_000_000, transcendentals=5_000_000
        ),
    )(args[0], args[1].T, args[2].T, *args[3:])


def solution(mesh):
    rows = P(("expert", "zero"), None)
    weight = P("expert", "zero", None)
    in_specs = (rows,) * 3 + (weight,) * 8
    return jax.shard_map(shards, mesh=mesh, in_specs=in_specs, out_specs=rows, check_vma=False)
```
